32 devices in a mesh: groups: 2 (over x), rows: 16 (over z, y, core).
Axes of the slice: x: 2, y: 2, z: 4, core: 2. Of those that a mesh axis runs over, the one named last changes fastest.
Arguments:
- embeddings: bfloat16 [16384, 128], P(('groups', 'rows')), parts along dimension 0, may hold values from -4 to 4
- noise_diag: float32 [16384], P(('groups', 'rows')), parts along dimension 0, may hold values from 0.2 to 2
- right_side: float32 [16, 16384], P(None, ('groups', 'rows')), parts along dimension 1, may hold values from -60 to 60
- pairs: int32 [2, 576], P(None, ('groups', 'rows')), parts along dimension 1, may hold values from 0 to 63, as said below
Outputs:
- solution: float32 [16, 16384], P(None, ('groups', 'rows')), parts along dimension 1
- residual: float32 [16, 16384], P(None, ('groups', 'rows')), parts along dimension 1
The draws below stay inside these ranges and needn't reach their ends.
There are 2 independent parts, one for each index of `groups`. The reference program is written for one: setup_inputs(seed, part) draws one part's arguments, and reference() takes and returns one part's arrays. A program takes and returns all parts, laid end to end along the dimension named above; each array names one. Nothing has to cross between parts.
Inputs may be any that keep to these rules, and one draw needn't show every extreme that they name: Block b is homed on device b // 4 of rows. The blocks form clusters of 8; every unordered pair of blocks of one cluster, a block with itself included, appears exactly once. The pairs of one device (its 18 columns) lie in one cluster, and no two different blocks that they name are homed on the same device.
All inputs are finite; a program needn't handle non-finite values.
Results may differ from the reference program's by a relative error of at most 0.035.
Values may be sent and summed in bfloat16 or wider, within the bound.
No kernel may reach another device: no remote copies, remote signals or barrier semaphores. Data moves between devices by JAX's collectives and lax.ppermute only.
A program may use at most 64 MiB of HBM per device.

```python
import math
import jax
import jax.numpy as jnp
import numpy as np
from jax import lax

EMB = 128
RHS = 16
BS = 128
BLK_DEV = 4
ITERS = 3
CLUSTER = 8
NBLOCKS = 64
ROWS_TOTAL = 8192
PAIR_DEV = 18


def draw_right_side(key, part):
    key = jax.random.fold_in(key, 5)
    key_base, key_rows, key_cols = jax.random.split(key, 3)
    row_scale = jnp.exp(jax.random.uniform(key_rows, (1, ROWS_TOTAL), jnp.float32) * math.log(10.0))
    col_scale = jnp.exp(jax.random.uniform(key_cols, (RHS, 1), jnp.float32) * math.log(10.0))
    rising = 1.0 + 2.0 * jnp.arange(ROWS_TOTAL, dtype=jnp.float32)[None, :] / (ROWS_TOTAL - 1)
    base = jax.random.truncated_normal(key_base, -4.0, 4.0, (RHS, ROWS_TOTAL), jnp.float32)
    return (base * row_scale * col_scale * rising / 20.0).astype(jnp.float32)


def draw_pairs(key, part):
    key = jax.random.fold_in(key, 9)
    devices = NBLOCKS // BLK_DEV
    key_slots, key_shuffle, key_owner = jax.random.split(key, 3)
    slot_keys = jax.random.split(key_slots, BLK_DEV)
    lines = jax.vmap(lambda one: jax.random.permutation(one, devices))(slot_keys)
    lines = lines * BLK_DEV + jnp.arange(BLK_DEV, dtype=jnp.int32)[:, None]
    clusters = lines.reshape(NBLOCKS // CLUSTER, CLUSTER)
    first, second = np.triu_indices(CLUSTER)
    left_block = clusters[:, first]
    right_block = clusters[:, second]
    shuffle_keys = jax.random.split(key_shuffle, NBLOCKS // CLUSTER)
    orders = jax.vmap(lambda one: jax.random.permutation(one, first.shape[0]))(shuffle_keys)
    left_block = jnp.take_along_axis(left_block, orders, axis=1).reshape(devices, PAIR_DEV)
    right_block = jnp.take_along_axis(right_block, orders, axis=1).reshape(devices, PAIR_DEV)
    owners = jax.random.permutation(key_owner, devices)
    left_block = left_block[owners]
    right_block = right_block[owners]
    return jnp.stack([left_block.reshape(-1), right_block.reshape(-1)]).astype(jnp.int32)


def shard_levels(key, dims, cuts, smallest, top_value):
    def one(dim, shards_of):
        draws = jax.random.uniform(jax.random.fold_in(jax.random.fold_in(key, 6), dim), (shards_of,), jnp.float32, smallest / len(cuts), top_value / len(cuts))
        return jnp.repeat(jnp.exp(draws), dims[dim] // shards_of).reshape((-1,) + (1,) * (len(dims) - dim - 1))

    gain = one(*cuts[0])
    for cut in cuts[1:]:
        gain = gain * one(*cut)
    return gain


def bell_draw(rng, shape, spread, limit, shards=(), kind=jnp.bfloat16):
    array = spread * jax.random.normal(rng, shape, jnp.float32)
    if shards:
        array = array * shard_levels(rng, shape, shards, -0.22, 0.18)
    return jnp.clip(array, -limit, limit).astype(kind)


def setup_inputs(seed: int = 0, part: int = 0) -> dict:
    keys = jax.random.split(jax.random.key(seed), 5)
    own_keys = jax.random.split(jax.random.fold_in(keys[4], part), 5)
    return {
        "embeddings": bell_draw(own_keys[0], (ROWS_TOTAL, EMB), 1.0, 4.0, ((0, 16),)),
        "noise_diag": jnp.clip(jnp.exp(math.log(2.0) - 2.3025851 * jax.random.uniform(own_keys[1], (ROWS_TOTAL,), jnp.float32) ** shard_levels(own_keys[1], (ROWS_TOTAL,), ((0, 16),), -0.2, 0.2)), 0.2, 2.0),
        "right_side": draw_right_side(jax.random.fold_in(jax.random.fold_in(keys[4], part), 71), part),
        "pairs": draw_pairs(jax.random.fold_in(jax.random.fold_in(keys[4], part), 71), part),
    }


def matern(inner, left_sq, right_sq, emb_width):
    length_scale = 0.5 * math.sqrt(2.0 * emb_width)
    distance_sq = jnp.maximum(left_sq[:, :, None] + right_sq[:, None, :] - 2.0 * inner, 0.0)
    scaled = jnp.sqrt(5.0 * distance_sq) / length_scale
    return ((1.0 + scaled + scaled * scaled / 3.0) * jnp.exp(-scaled)).astype(jnp.bfloat16)

def reference(embeddings, noise_diag, right_side, pairs):
    blocks = embeddings.reshape(NBLOCKS, BS, EMB)
    squares = lax.optimization_barrier(jnp.sum(jnp.square(blocks.astype(jnp.float32)), axis=-1))
    left_idx = pairs[0].reshape(-1, PAIR_DEV)
    right_idx = pairs[1].reshape(-1, PAIR_DEV)

    def operate(vector):
        rounded = vector.astype(jnp.bfloat16).reshape(RHS, NBLOCKS, BS)

        def accumulate(totals, item):
            first_idx, second_idx = item
            inner = jnp.einsum('gae,gbe->gab', blocks[first_idx].astype(jnp.float32), blocks[second_idx].astype(jnp.float32), precision=lax.Precision.HIGHEST)
            kernel = matern(inner, squares[first_idx], squares[second_idx], EMB).astype(jnp.float32)
            toward_left = jnp.einsum('gab,rgb->rga', kernel, rounded[:, second_idx].astype(jnp.float32), precision=lax.Precision.HIGHEST)
            toward_right = jnp.einsum('gab,rga->rgb', kernel, rounded[:, first_idx].astype(jnp.float32), precision=lax.Precision.HIGHEST)
            off_diagonal = (first_idx != second_idx).astype(jnp.float32)
            toward_right = toward_right * off_diagonal[None, :, None]
            totals = totals.at[:, first_idx].add(toward_left).at[:, second_idx].add(toward_right)
            return (totals, None)
        totals, _ = lax.scan(accumulate, jnp.zeros((RHS, NBLOCKS, BS), jnp.float32), (left_idx, right_idx))
        return noise_diag[None, :] * vector + totals.reshape(RHS, ROWS_TOTAL)
    solution = jnp.zeros_like(right_side)
    residual = right_side
    direction = right_side
    norm_now = lax.optimization_barrier(jnp.sum(residual * residual, axis=1))
    for iteration in range(ITERS):
        image = operate(direction)
        step_len = norm_now / lax.optimization_barrier(jnp.sum(direction * image, axis=1))
        solution = solution + step_len[:, None] * direction
        residual = residual - step_len[:, None] * image
        norm_next = lax.optimization_barrier(jnp.sum(residual * residual, axis=1))
        direction = residual + (norm_next / norm_now)[:, None] * direction
        norm_now = norm_next
    return (solution, residual)
```

```python
import functools
import math

import jax
import jax.numpy as jnp
from jax import lax
from jax.experimental import pallas as pl
from jax.experimental.pallas import tpu as pltpu
from jax.sharding import PartitionSpec as P

BS = 128
BLK_DEV = 4
STEPS = 3
LANES = 128
F32 = jnp.float32
BF16 = jnp.bfloat16


def split3(value):
    high = value.astype(BF16).astype(F32)
    rest = value - high
    middle = rest.astype(BF16).astype(F32)
    return high, middle, rest - middle


def plan_kernel(team, size, count, pairs_ref, emb_ref, noise_ref, rhs_ref, packed_ref, info_ref):
    devices = pairs_ref.shape[0]
    width = max(LANES, devices * BLK_DEV)
    rhs = rhs_ref.shape[0]
    me = lax.axis_index("rows")
    block_id = lax.broadcasted_iota(jnp.int32, (devices, width), 1)
    named = jnp.zeros((devices, width), F32)
    for side in range(2):
        ids = pairs_ref[:, side, :]
        for item in range(count):
            named = jnp.where(ids[:, item : item + 1] == block_id, 1.0, named)
    named = named.astype(BF16)
    together = lax.dot_general(named, named, (((1,), (1,)), ((), ())), preferred_element_type=F32)
    together = together > 0.0
    if team > 2:
        link = together.astype(F32).astype(BF16)
        together = jnp.dot(link, link, preferred_element_type=F32) > 0.0
    link = together.astype(F32)
    members = jnp.dot(link.astype(BF16), named, preferred_element_type=F32) > 0.0
    down = lax.broadcasted_iota(jnp.int32, (devices, devices), 0).astype(F32)
    across = lax.broadcasted_iota(jnp.int32, (devices, devices), 1).astype(F32)
    far = float(devices)
    leader_down = jnp.min(jnp.where(together, across, far), axis=1, keepdims=True)
    leader_across = jnp.min(jnp.where(together, down, far), axis=0, keepdims=True)
    first = leader_across == across
    rank = jnp.sum(
        jnp.where(jnp.logical_and(first, across < leader_down), 1.0, 0.0), axis=1, keepdims=True
    )
    label = jnp.max(jnp.where(members, rank, -1.0), axis=0, keepdims=True)

    lane = lax.broadcasted_iota(jnp.int32, (1, width), 1)
    row = lax.broadcasted_iota(jnp.int32, (16, BS), 0)
    spots = []
    for slot in range(BLK_DEV):
        mine = jnp.sum(jnp.where(lane == me * BLK_DEV + slot, label, 0.0)).astype(jnp.int32)
        spots.append(mine)
        rows = slice(slot * BS, (slot + 1) * BS)
        packed_ref[mine, 0:BS, :] = emb_ref[rows, :]
        vector = rhs_ref[:, rows]
        high = vector.astype(BF16)
        packed_ref[mine, BS : BS + rhs, :] = high
        packed_ref[mine, BS + rhs : BS + 2 * rhs, :] = (vector - high.astype(F32)).astype(BF16)
        top, middle, low = split3(noise_ref[slot : slot + 1, :])
        noise = jnp.where(row == 0, top, jnp.where(row == 1, middle, jnp.where(row == 2, low, 0.0)))
        packed_ref[mine, BS + 2 * rhs : BS + 2 * rhs + 16, :] = noise.astype(BF16)

    height = info_ref.shape[0] - 8
    hit = jnp.where(label == (me // team).astype(F32), 1.0, 0.0)
    hit = jnp.broadcast_to(hit, (height, width))
    upper = lax.broadcasted_iota(jnp.int32, (width, width), 0) <= lax.broadcasted_iota(
        jnp.int32, (width, width), 1
    )
    before = jnp.dot(
        hit.astype(BF16), upper.astype(F32).astype(BF16), preferred_element_type=F32
    )
    place = lax.broadcasted_iota(jnp.int32, (height, width), 0).astype(F32) + 1.0
    ids = lax.broadcasted_iota(jnp.int32, (height, width), 1).astype(F32)
    chosen = jnp.where(jnp.logical_and(hit > 0.0, before == place), ids, 0.0)
    order = jnp.sum(chosen, axis=1, keepdims=True).astype(jnp.int32)
    info_ref[0:height, :] = jnp.broadcast_to(order, (height, LANES))
    line = lax.broadcasted_iota(jnp.int32, (8, LANES), 0)
    own = jnp.zeros((8, LANES), jnp.int32)
    for slot in range(BLK_DEV):
        own = jnp.where(line == slot, spots[slot], own)
    info_ref[height : height + 8, :] = own


def krylov_kernel(team, size, emb_width, info_ref, *refs):
    parts = refs[:team]
    out_ref, left, right, gram, start, noise = refs[team:]
    order = size * BS
    rhs = start.shape[0]
    mine = lax.axis_index("rows") % team
    lane = lax.broadcasted_iota(jnp.int32, (BS, LANES), 1)
    line = lax.broadcasted_iota(jnp.int32, (LANES, BS), 0)
    spots = []
    for place in range(size):
        home = info_ref[place, 0] // BLK_DEV
        member = home % team
        slot = home // team
        spots.append((member, slot))
        tile = parts[0][slot]
        for other in range(1, team):
            tile = jnp.where(member ^ mine == other, parts[other][slot], tile)
        rows = slice(place * BS, (place + 1) * BS)
        emb = tile[:BS].astype(F32)
        turned = emb.T
        left[rows, :emb_width] = tile[:BS]
        right[:emb_width, rows] = (turned * -2.0).astype(BF16)
        top, middle, low = split3(jnp.sum(emb * emb, axis=1, keepdims=True))
        extra = jnp.where(lane < 2 * 3, 1.0, 0.0)
        extra = jnp.where(lane == 2, low, extra)
        extra = jnp.where(lane == 1, middle, extra)
        left[rows, emb_width:] = jnp.where(lane == 0, top, extra).astype(BF16)
        top, middle, low = split3(jnp.sum(turned * turned, axis=0, keepdims=True))
        extra = jnp.where(line < 3, 1.0, 0.0)
        extra = jnp.where(line == 5, low, extra)
        extra = jnp.where(line == 4, middle, extra)
        right[emb_width:, rows] = jnp.where(line == 3, top, extra).astype(BF16)
        start[:, rows] = tile[BS : BS + rhs].astype(F32) + tile[BS + rhs : BS + 2 * rhs].astype(F32)
        noise[:, rows] = jnp.sum(
            tile[BS + 2 * rhs : BS + 2 * rhs + 16].astype(F32), axis=0, keepdims=True
        )

    length_scale = 0.5 * math.sqrt(2.0 * emb_width)
    chunk = 256
    for column in range(0, order, chunk):
        columns = slice(column, column + chunk)
        distance_sq = jnp.dot(left[...], right[:, columns], preferred_element_type=F32)
        distance_sq = jnp.maximum(distance_sq, 1e-12)
        scaled = distance_sq * lax.rsqrt(distance_sq) * (math.sqrt(5.0) / length_scale)
        value = ((scaled * (1.0 / 3.0) + 1.0) * scaled + 1.0) * jnp.exp(-scaled)
        gram[:, columns] = value.astype(BF16)

    def unit(vector):
        norm = jnp.sqrt(jnp.sum(vector * vector, axis=1, keepdims=True))
        return norm, vector * jnp.where(norm > 0.0, 1.0 / norm, 0.0)

    norm, basis = unit(start[...])
    basis = [basis]
    numbers = [norm]
    for step in range(STEPS):
        image = noise[...] * basis[step] + jnp.dot(
            basis[step].astype(BF16), gram[...], preferred_element_type=F32
        )
        dots = [jnp.sum(one * image, axis=1, keepdims=True) for one in basis]
        for one, dot in zip(basis, dots, strict=True):
            image = image - dot * one
        norm, fresh = unit(image)
        basis.append(fresh)
        numbers += dots + [norm]

    spot = lax.broadcasted_iota(jnp.int32, (rhs, LANES), 1)
    table = jnp.zeros((rhs, LANES), F32)
    for index, number in enumerate(numbers):
        table = jnp.where(spot == index, number, table)
    top, middle, low = split3(table)
    table = top + pltpu.roll(middle, 16, 1) + pltpu.roll(low, 32, 1)
    table = table.astype(BF16)
    for slot in range(out_ref.shape[0]):
        out_ref[slot, STEPS * rhs : (STEPS + 1) * rhs, :] = table
    for place, (member, slot) in enumerate(spots):

        @pl.when(member == mine)
        def _(place=place, slot=slot):
            for step in range(STEPS):
                out_ref[slot, step * rhs : (step + 1) * rhs, :] = basis[step + 1][
                    :, place * BS : (place + 1) * BS
                ].astype(BF16)


def combine_kernel(height, info_ref, back_ref, rhs_ref, solution_ref, residual_ref, table, coefs):
    clusters = back_ref.shape[0]
    rhs = rhs_ref.shape[0]
    for cluster in range(clusters):
        part = back_ref[cluster, STEPS * rhs : (STEPS + 1) * rhs, :].astype(F32)
        part = part + pltpu.roll(part, LANES - 16, 1) + pltpu.roll(part, LANES - 32, 1)
        wide = jnp.concatenate([part, jnp.zeros((LANES - rhs, LANES), F32)], axis=0)
        table[cluster] = wide.T[:16, :]
    rows = [table[:, index, :] for index in range(1 + sum(range(2, STEPS + 2)))]
    norm = rows[0]
    columns, at = [], 1
    for step in range(STEPS):
        columns.append(rows[at : at + step + 2])
        at += step + 2
    zero = jnp.zeros_like(norm)
    solution = [zero] * STEPS
    residual = [norm] + [zero] * STEPS
    direction = [norm] + [zero] * STEPS

    def total(values):
        return jnp.sum(functools.reduce(jnp.add, values), axis=0, keepdims=True)

    norm_now = total([norm * norm])
    for step in range(STEPS):
        image = []
        for out in range(step + 2):
            image.append(
                functools.reduce(
                    jnp.add,
                    [columns[k][out] * direction[k] for k in range(max(out - 1, 0), step + 1)],
                )
            )
        step_len = norm_now / total([direction[k] * image[k] for k in range(step + 1)])
        for k in range(step + 1):
            solution[k] = solution[k] + step_len * direction[k]
        for k in range(step + 2):
            residual[k] = residual[k] - step_len * image[k]
        norm_next = total([residual[k] * residual[k] for k in range(step + 2)])
        ratio = norm_next / norm_now
        for k in range(step + 2):
            direction[k] = residual[k] + ratio * direction[k]
        norm_now = norm_next
    scale = jnp.where(norm > 0.0, 1.0 / norm, 0.0)
    solution[0] = solution[0] * scale
    residual[0] = residual[0] * scale
    all_coefs = solution + residual
    kinds = len(all_coefs)
    for index, one in enumerate(all_coefs):
        table[:, index, :] = one
    coefs[...] = jnp.zeros_like(coefs)
    labels = [info_ref[height + slot, 0] for slot in range(BLK_DEV)]
    for slot in range(BLK_DEV):
        coefs[slot * 16 : (slot + 1) * 16, :] = table[labels[slot]]
    turned = coefs[...].T
    for slot in range(BLK_DEV):
        block = slice(slot * BS, (slot + 1) * BS)
        vectors = [rhs_ref[:, block]] + [
            back_ref[labels[slot], step * rhs : (step + 1) * rhs, :].astype(F32)
            for step in range(STEPS)
        ]
        weights = [turned[:rhs, slot * 16 + k : slot * 16 + k + 1] for k in range(kinds)]
        solution_ref[:, block] = functools.reduce(
            jnp.add, [weights[k] * vectors[k] for k in range(STEPS)]
        )
        residual_ref[:, block] = functools.reduce(
            jnp.add, [weights[STEPS + k] * vectors[k] for k in range(STEPS + 1)]
        )


def local(embeddings, noise_diag, right_side, pairs):
    devices = lax.axis_size("rows")
    emb_width = embeddings.shape[1]
    rhs, local_rows = right_side.shape
    count = pairs.shape[1]
    size = count // 2 - 1
    team = size // BLK_DEV
    clusters = devices // team
    height = max(8, size)
    slot_rows = BS + 2 * rhs + 16
    vmem = pl.BlockSpec(memory_space=pltpu.VMEM)
    smem = pl.BlockSpec(memory_space=pltpu.SMEM)
    params = pltpu.CompilerParams(vmem_limit_bytes=48 * 1024 * 1024)

    mine = jnp.pad(pairs, ((0, 6), (0, LANES - count)))
    every = jnp.broadcast_to(mine[None], (devices, 8, LANES))
    every = lax.all_to_all(every, "rows", split_axis=0, concat_axis=0, tiled=True)
    packed, info = pl.pallas_call(
        functools.partial(plan_kernel, team, size, count),
        out_shape=(
            jax.ShapeDtypeStruct((clusters, slot_rows, LANES), BF16),
            jax.ShapeDtypeStruct((height + 8, LANES), jnp.int32),
        ),
        in_specs=[vmem] * 4,
        out_specs=(vmem, vmem),
        compiler_params=params,
        name="plan",
    )(every, embeddings, noise_diag.reshape(BLK_DEV, BS), right_side)
    same = [[lead * team + member for lead in range(clusters)] for member in range(team)]
    parts = [
        lax.all_to_all(
            packed, "rows", split_axis=0, concat_axis=0, tiled=True, axis_index_groups=same
        )
    ]
    reach = 1
    while reach < team:
        parts = parts + [
            lax.ppermute(one, "rows", [(i, i ^ reach) for i in range(devices)]) for one in parts
        ]
        reach *= 2
    order = size * BS
    back = pl.pallas_call(
        functools.partial(krylov_kernel, team, size, emb_width),
        out_shape=jax.ShapeDtypeStruct((clusters, (STEPS + 1) * rhs, LANES), BF16),
        in_specs=[smem] + [vmem] * team,
        out_specs=vmem,
        scratch_shapes=[
            pltpu.VMEM((order, 2 * emb_width), BF16),
            pltpu.VMEM((2 * emb_width, order), BF16),
            pltpu.VMEM((order, order), BF16),
            pltpu.VMEM((rhs, order), F32),
            pltpu.VMEM((1, order), F32),
        ],
        compiler_params=params,
        name="krylov",
    )(info, *parts)
    back = lax.all_to_all(
        back, "rows", split_axis=0, concat_axis=0, tiled=True, axis_index_groups=same
    )
    return pl.pallas_call(
        functools.partial(combine_kernel, height),
        out_shape=(
            jax.ShapeDtypeStruct((rhs, local_rows), F32),
            jax.ShapeDtypeStruct((rhs, local_rows), F32),
        ),
        in_specs=[smem, vmem, vmem],
        out_specs=(vmem, vmem),
        scratch_shapes=[
            pltpu.VMEM((clusters, 16, LANES), F32),
            pltpu.VMEM((LANES, LANES), F32),
        ],
        compiler_params=params,
        name="combine",
    )(info, back, right_side)


def solution(mesh):
    in_specs = (
        P(("groups", "rows"), None),
        P(("groups", "rows")),
        P(None, ("groups", "rows")),
        P(None, ("groups", "rows")),
    )
    out_specs = (P(None, ("groups", "rows")), P(None, ("groups", "rows")))
    return jax.shard_map(local, mesh=mesh, in_specs=in_specs, out_specs=out_specs, check_vma=False)
```

```python
import functools
import math

import jax
import jax.numpy as jnp
from jax import lax
from jax.experimental import pallas as pl
from jax.experimental.pallas import tpu as pltpu
from jax.sharding import PartitionSpec as P

BS = 128
BLK_DEV = 4
STEPS = 3
LANES = 128
F32 = jnp.float32
BF16 = jnp.bfloat16


def split3(value):
    high = value.astype(BF16).astype(F32)
    rest = value - high
    middle = rest.astype(BF16).astype(F32)
    return high, middle, rest - middle


def announce_kernel(pairs_ref, noise_ref, out_ref):
    devices, height, _ = out_ref.shape
    count = pairs_ref.shape[1]
    block_id = sum(
        lax.broadcasted_iota(jnp.int32, (height, LANES), dim) * step for dim, step in ((0, LANES), (1, 1))
    )
    tile = jnp.zeros((height, LANES), F32)
    for side in range(2):
        for item in range(count):
            tile = jnp.where(block_id == pairs_ref[side, item], 1.0, tile)
    line = lax.broadcasted_iota(jnp.int32, (height, LANES), 0)
    for slot in range(BLK_DEV):
        tile = jnp.where(line == height - BLK_DEV + slot, noise_ref[slot : slot + 1, :], tile)
    for device in range(devices):
        out_ref[device] = tile


def plan_kernel(team, size, news_ref, emb_ref, rhs_ref, packed_ref, info_ref):
    devices = news_ref.shape[0]
    width = pl.cdiv(devices * BLK_DEV, LANES) * LANES
    rhs = rhs_ref.shape[0]
    me = lax.axis_index("rows")
    named = jnp.concatenate([news_ref[:, line, :] for line in range(width // LANES)], axis=1)
    named = named.astype(BF16)
    together = lax.dot_general(named, named, (((1,), (1,)), ((), ())), preferred_element_type=F32)
    together = together > 0.0
    if team > 2:
        link = together.astype(F32).astype(BF16)
        together = jnp.dot(link, link, preferred_element_type=F32) > 0.0
    link = together.astype(F32)
    members = jnp.dot(link.astype(BF16), named, preferred_element_type=F32) > 0.0
    down = lax.broadcasted_iota(jnp.int32, (devices, devices), 0).astype(F32)
    across = lax.broadcasted_iota(jnp.int32, (devices, devices), 1).astype(F32)
    far = float(devices)
    leader_down = jnp.min(jnp.where(together, across, far), axis=1, keepdims=True)
    leader_across = jnp.min(jnp.where(together, down, far), axis=0, keepdims=True)
    first = leader_across == across
    rank = jnp.sum(
        jnp.where(jnp.logical_and(first, across < leader_down), 1.0, 0.0), axis=1, keepdims=True
    )
    label = jnp.max(jnp.where(members, rank, -1.0), axis=0, keepdims=True)

    lane = lax.broadcasted_iota(jnp.int32, (1, width), 1)
    spots = []
    for slot in range(BLK_DEV):
        mine = jnp.sum(jnp.where(lane == me * BLK_DEV + slot, label, 0.0)).astype(jnp.int32)
        spots.append(mine)
        rows = slice(slot * BS, (slot + 1) * BS)
        packed_ref[mine, 0:BS, :] = emb_ref[rows, :]
        packed_ref[mine, BS : BS + rhs, :] = rhs_ref[:, rows].astype(BF16)

    height = info_ref.shape[0] - 8
    hit = jnp.where(label == (me // team).astype(F32), 1.0, 0.0)
    hit = jnp.broadcast_to(hit, (height, width))
    upper = lax.broadcasted_iota(jnp.int32, (width, width), 0) <= lax.broadcasted_iota(
        jnp.int32, (width, width), 1
    )
    before = jnp.dot(
        hit.astype(BF16), upper.astype(F32).astype(BF16), preferred_element_type=F32
    )
    place = lax.broadcasted_iota(jnp.int32, (height, width), 0).astype(F32) + 1.0
    ids = lax.broadcasted_iota(jnp.int32, (height, width), 1).astype(F32)
    chosen = jnp.where(jnp.logical_and(hit > 0.0, before == place), ids, 0.0)
    order = jnp.sum(chosen, axis=1, keepdims=True).astype(jnp.int32)
    info_ref[0:height, :] = jnp.broadcast_to(order, (height, LANES))
    line = lax.broadcasted_iota(jnp.int32, (8, LANES), 0)
    own = jnp.zeros((8, LANES), jnp.int32)
    for slot in range(BLK_DEV):
        own = jnp.where(line == slot, spots[slot], own)
    info_ref[height : height + 8, :] = own


def krylov_kernel(team, size, emb_width, info_ref, news_ref, *refs):
    parts = refs[:team]
    out_ref, left, right, gram, start, noise = refs[team:]
    diagonal_at = news_ref.shape[1] - BLK_DEV
    order = size * BS
    rhs = start.shape[0]
    mine = lax.axis_index("rows") % team
    lane = lax.broadcasted_iota(jnp.int32, (BS, LANES), 1)
    line = lax.broadcasted_iota(jnp.int32, (LANES, BS), 0)
    spots = []
    for place in range(size):
        home = info_ref[place, 0] // BLK_DEV
        member = home % team
        slot = home // team
        spots.append((member, slot))
        tile = parts[0][slot]
        for other in range(1, team):
            tile = jnp.where(member ^ mine == other, parts[other][slot], tile)
        rows = slice(place * BS, (place + 1) * BS)
        emb = tile[:BS].astype(F32)
        turned = emb.T
        left[rows, :emb_width] = tile[:BS]
        right[:emb_width, rows] = (turned * -2.0).astype(BF16)
        top, middle, low = split3(jnp.sum(emb * emb, axis=1, keepdims=True))
        extra = jnp.where(lane < 2 * 3, 1.0, 0.0)
        extra = jnp.where(lane == 2, low, extra)
        extra = jnp.where(lane == 1, middle, extra)
        left[rows, emb_width:] = jnp.where(lane == 0, top, extra).astype(BF16)
        top, middle, low = split3(jnp.sum(turned * turned, axis=0, keepdims=True))
        extra = jnp.where(line < 3, 1.0, 0.0)
        extra = jnp.where(line == 5, low, extra)
        extra = jnp.where(line == 4, middle, extra)
        right[emb_width:, rows] = jnp.where(line == 3, top, extra).astype(BF16)
        start[:, rows] = tile[BS : BS + rhs].astype(F32)
        noise[:, rows] = news_ref[home, pl.ds(diagonal_at + info_ref[place, 0] % BLK_DEV, 1), :]

    length_scale = 0.5 * math.sqrt(2.0 * emb_width)
    chunk = 256
    for column in range(0, order, chunk):
        columns = slice(column, column + chunk)
        distance_sq = jnp.dot(left[...], right[:, columns], preferred_element_type=F32)
        distance_sq = jnp.maximum(distance_sq, 1e-12)
        scaled = distance_sq * lax.rsqrt(distance_sq) * (math.sqrt(5.0) / length_scale)
        value = ((scaled * (1.0 / 3.0) + 1.0) * scaled + 1.0) * jnp.exp(-scaled)
        gram[:, columns] = value.astype(BF16)

    def unit(vector):
        norm = jnp.sqrt(jnp.sum(vector * vector, axis=1, keepdims=True))
        return norm, vector * jnp.where(norm > 0.0, 1.0 / norm, 0.0)

    norm, basis = unit(start[...])
    basis = [basis]
    numbers = [norm]
    for step in range(STEPS):
        image = noise[...] * basis[step] + jnp.dot(
            basis[step].astype(BF16), gram[...], preferred_element_type=F32
        )
        dots = [jnp.sum(one * image, axis=1, keepdims=True) for one in basis]
        for one, dot in zip(basis, dots, strict=True):
            image = image - dot * one
        norm, fresh = unit(image)
        basis.append(fresh)
        numbers += dots + [norm]

    spot = lax.broadcasted_iota(jnp.int32, (rhs, LANES), 1)
    table = jnp.zeros((rhs, LANES), F32)
    for index, number in enumerate(numbers):
        table = jnp.where(spot == index, number, table)
    top, middle, low = split3(table)
    table = top + pltpu.roll(middle, 16, 1) + pltpu.roll(low, 32, 1)
    table = table.astype(BF16)
    for slot in range(out_ref.shape[0]):
        out_ref[slot, STEPS * rhs : (STEPS + 1) * rhs, :] = table
    for place, (member, slot) in enumerate(spots):

        @pl.when(member == mine)
        def _(place=place, slot=slot):
            for step in range(STEPS):
                out_ref[slot, step * rhs : (step + 1) * rhs, :] = basis[step + 1][
                    :, place * BS : (place + 1) * BS
                ].astype(BF16)


def combine_kernel(height, info_ref, back_ref, rhs_ref, solution_ref, residual_ref, table, coefs):
    clusters = back_ref.shape[0]
    rhs = rhs_ref.shape[0]
    for cluster in range(clusters):
        part = back_ref[cluster, STEPS * rhs : (STEPS + 1) * rhs, :].astype(F32)
        part = part + pltpu.roll(part, LANES - 16, 1) + pltpu.roll(part, LANES - 32, 1)
        wide = jnp.concatenate([part, jnp.zeros((LANES - rhs, LANES), F32)], axis=0)
        table[cluster] = wide.T[:16, :]
    rows = [table[:, index, :] for index in range(1 + sum(range(2, STEPS + 2)))]
    norm = rows[0]
    columns, at = [], 1
    for step in range(STEPS):
        columns.append(rows[at : at + step + 2])
        at += step + 2
    zero = jnp.zeros_like(norm)
    solution = [zero] * STEPS
    residual = [norm] + [zero] * STEPS
    direction = [norm] + [zero] * STEPS

    def total(values):
        return jnp.sum(functools.reduce(jnp.add, values), axis=0, keepdims=True)

    norm_now = total([norm * norm])
    for step in range(STEPS):
        image = []
        for out in range(step + 2):
            image.append(
                functools.reduce(
                    jnp.add,
                    [columns[k][out] * direction[k] for k in range(max(out - 1, 0), step + 1)],
                )
            )
        step_len = norm_now / total([direction[k] * image[k] for k in range(step + 1)])
        for k in range(step + 1):
            solution[k] = solution[k] + step_len * direction[k]
        for k in range(step + 2):
            residual[k] = residual[k] - step_len * image[k]
        norm_next = total([residual[k] * residual[k] for k in range(step + 2)])
        ratio = norm_next / norm_now
        for k in range(step + 2):
            direction[k] = residual[k] + ratio * direction[k]
        norm_now = norm_next
    scale = jnp.where(norm > 0.0, 1.0 / norm, 0.0)
    solution[0] = solution[0] * scale
    residual[0] = residual[0] * scale
    all_coefs = solution + residual
    kinds = len(all_coefs)
    for index, one in enumerate(all_coefs):
        table[:, index, :] = one
    coefs[...] = jnp.zeros_like(coefs)
    labels = [info_ref[height + slot, 0] for slot in range(BLK_DEV)]
    for slot in range(BLK_DEV):
        coefs[slot * 16 : (slot + 1) * 16, :] = table[labels[slot]]
    turned = coefs[...].T
    for slot in range(BLK_DEV):
        block = slice(slot * BS, (slot + 1) * BS)
        vectors = [rhs_ref[:, block]] + [
            back_ref[labels[slot], step * rhs : (step + 1) * rhs, :].astype(F32)
            for step in range(STEPS)
        ]
        weights = [turned[:rhs, slot * 16 + k : slot * 16 + k + 1] for k in range(kinds)]
        solution_ref[:, block] = functools.reduce(
            jnp.add, [weights[k] * vectors[k] for k in range(STEPS)]
        )
        residual_ref[:, block] = functools.reduce(
            jnp.add, [weights[STEPS + k] * vectors[k] for k in range(STEPS + 1)]
        )


def local(embeddings, noise_diag, right_side, pairs):
    devices = lax.axis_size("rows")
    emb_width = embeddings.shape[1]
    rhs, local_rows = right_side.shape
    count = pairs.shape[1]
    size = count // 2 - 1
    team = size // BLK_DEV
    clusters = devices // team
    height = max(8, size)
    slot_rows = BS + rhs
    vmem = pl.BlockSpec(memory_space=pltpu.VMEM)
    smem = pl.BlockSpec(memory_space=pltpu.SMEM)
    params = pltpu.CompilerParams(vmem_limit_bytes=48 * 1024 * 1024)

    news_rows = 8 * pl.cdiv(BLK_DEV + pl.cdiv(devices * BLK_DEV, LANES), 8)
    every = pl.pallas_call(
        announce_kernel,
        out_shape=jax.ShapeDtypeStruct((devices, news_rows, LANES), F32),
        in_specs=[smem, vmem],
        out_specs=vmem,
        compiler_params=params,
        name="announce",
    )(pairs, noise_diag.reshape(BLK_DEV, BS))
    every = lax.all_to_all(every, "rows", split_axis=0, concat_axis=0, tiled=True)
    packed, info = pl.pallas_call(
        functools.partial(plan_kernel, team, size),
        out_shape=(
            jax.ShapeDtypeStruct((clusters, slot_rows, LANES), BF16),
            jax.ShapeDtypeStruct((height + 8, LANES), jnp.int32),
        ),
        in_specs=[vmem] * 3,
        out_specs=(vmem, vmem),
        compiler_params=params,
        name="plan",
    )(every, embeddings, right_side)
    same = [[lead * team + member for lead in range(clusters)] for member in range(team)]
    parts = [
        lax.all_to_all(
            packed, "rows", split_axis=0, concat_axis=0, tiled=True, axis_index_groups=same
        )
    ]
    reach = 1
    while reach < team:
        parts = parts + [
            lax.ppermute(one, "rows", [(i, i ^ reach) for i in range(devices)]) for one in parts
        ]
        reach *= 2
    order = size * BS
    back = pl.pallas_call(
        functools.partial(krylov_kernel, team, size, emb_width),
        out_shape=jax.ShapeDtypeStruct((clusters, (STEPS + 1) * rhs, LANES), BF16),
        in_specs=[smem] + [vmem] * (team + 1),
        out_specs=vmem,
        scratch_shapes=[
            pltpu.VMEM((order, 2 * emb_width), BF16),
            pltpu.VMEM((2 * emb_width, order), BF16),
            pltpu.VMEM((order, order), BF16),
            pltpu.VMEM((rhs, order), F32),
            pltpu.VMEM((1, order), F32),
        ],
        compiler_params=params,
        name="krylov",
    )(info, every, *parts)
    back = lax.all_to_all(
        back, "rows", split_axis=0, concat_axis=0, tiled=True, axis_index_groups=same
    )
    return pl.pallas_call(
        functools.partial(combine_kernel, height),
        out_shape=(
            jax.ShapeDtypeStruct((rhs, local_rows), F32),
            jax.ShapeDtypeStruct((rhs, local_rows), F32),
        ),
        in_specs=[smem, vmem, vmem],
        out_specs=(vmem, vmem),
        scratch_shapes=[
            pltpu.VMEM((clusters, 16, LANES), F32),
            pltpu.VMEM((LANES, LANES), F32),
        ],
        compiler_params=params,
        name="combine",
    )(info, back, right_side)


def solution(mesh):
    in_specs = (
        P(("groups", "rows"), None),
        P(("groups", "rows")),
        P(None, ("groups", "rows")),
        P(None, ("groups", "rows")),
    )
    out_specs = (P(None, ("groups", "rows")), P(None, ("groups", "rows")))
    return jax.shard_map(local, mesh=mesh, in_specs=in_specs, out_specs=out_specs, check_vma=False)
```

```python
import functools
import math

import jax
import jax.numpy as jnp
from jax import lax
from jax.experimental import pallas as pl
from jax.experimental.pallas import tpu as pltpu
from jax.sharding import PartitionSpec as P

BS = 128
BLK_DEV = 4
STEPS = 3
LANES = 128
F32 = jnp.float32
BF16 = jnp.bfloat16


def split3(value):
    high = value.astype(BF16).astype(F32)
    rest = value - high
    middle = rest.astype(BF16).astype(F32)
    return high, middle, rest - middle


def announce_kernel(pairs_hbm, noise_hbm, out_ref, pairs_ref, noise_ref, arrived):
    fetches = [
        pltpu.make_async_copy(pairs_hbm, pairs_ref, arrived.at[0]),
        pltpu.make_async_copy(noise_hbm, noise_ref, arrived.at[1]),
    ]
    for fetch in fetches:
        fetch.start()
    devices, height, _ = out_ref.shape
    count = pairs_ref.shape[1]
    block_id = sum(
        lax.broadcasted_iota(jnp.int32, (height, LANES), dim) * step for dim, step in ((0, LANES), (1, 1))
    )
    tile = jnp.zeros((height, LANES), F32)
    fetches[0].wait()
    for side in range(2):
        for item in range(count):
            tile = jnp.where(block_id == pairs_ref[side, item], 1.0, tile)
    line = lax.broadcasted_iota(jnp.int32, (height, LANES), 0)
    fetches[1].wait()
    for slot in range(BLK_DEV):
        tile = jnp.where(line == height - BLK_DEV + slot, noise_ref[slot : slot + 1, :], tile)
    for device in range(devices):
        out_ref[device] = tile


def plan_kernel(team, size, news_ref, emb_ref, rhs_ref, packed_ref, info_ref):
    devices = news_ref.shape[0]
    width = pl.cdiv(devices * BLK_DEV, LANES) * LANES
    rhs = rhs_ref.shape[0]
    me = lax.axis_index("rows")
    named = jnp.concatenate([news_ref[:, line, :] for line in range(width // LANES)], axis=1)
    named = named.astype(BF16)
    together = lax.dot_general(named, named, (((1,), (1,)), ((), ())), preferred_element_type=F32)
    together = together > 0.0
    if team > 2:
        link = together.astype(F32).astype(BF16)
        together = jnp.dot(link, link, preferred_element_type=F32) > 0.0
    link = together.astype(F32)
    members = jnp.dot(link.astype(BF16), named, preferred_element_type=F32) > 0.0
    down = lax.broadcasted_iota(jnp.int32, (devices, devices), 0).astype(F32)
    across = lax.broadcasted_iota(jnp.int32, (devices, devices), 1).astype(F32)
    far = float(devices)
    leader_down = jnp.min(jnp.where(together, across, far), axis=1, keepdims=True)
    leader_across = jnp.min(jnp.where(together, down, far), axis=0, keepdims=True)
    first = leader_across == across
    rank = jnp.sum(
        jnp.where(jnp.logical_and(first, across < leader_down), 1.0, 0.0), axis=1, keepdims=True
    )
    label = jnp.max(jnp.where(members, rank, -1.0), axis=0, keepdims=True)

    lane = lax.broadcasted_iota(jnp.int32, (1, width), 1)
    spots = []
    for slot in range(BLK_DEV):
        mine = jnp.sum(jnp.where(lane == me * BLK_DEV + slot, label, 0.0)).astype(jnp.int32)
        spots.append(mine)
        rows = slice(slot * BS, (slot + 1) * BS)
        packed_ref[mine, 0:BS, :] = emb_ref[rows, :]
        packed_ref[mine, BS : BS + rhs, :] = rhs_ref[:, rows].astype(BF16)

    height = info_ref.shape[0] - 8
    hit = jnp.where(label == (me // team).astype(F32), 1.0, 0.0)
    hit = jnp.broadcast_to(hit, (height, width))
    upper = lax.broadcasted_iota(jnp.int32, (width, width), 0) <= lax.broadcasted_iota(
        jnp.int32, (width, width), 1
    )
    before = jnp.dot(
        hit.astype(BF16), upper.astype(F32).astype(BF16), preferred_element_type=F32
    )
    place = lax.broadcasted_iota(jnp.int32, (height, width), 0).astype(F32) + 1.0
    ids = lax.broadcasted_iota(jnp.int32, (height, width), 1).astype(F32)
    chosen = jnp.where(jnp.logical_and(hit > 0.0, before == place), ids, 0.0)
    order = jnp.sum(chosen, axis=1, keepdims=True).astype(jnp.int32)
    info_ref[0:height, :] = jnp.broadcast_to(order, (height, LANES))
    line = lax.broadcasted_iota(jnp.int32, (8, LANES), 0)
    own = jnp.zeros((8, LANES), jnp.int32)
    for slot in range(BLK_DEV):
        own = jnp.where(line == slot, spots[slot], own)
    info_ref[height : height + 8, :] = own


def krylov_kernel(team, size, emb_width, info_ref, news_ref, *refs):
    parts = refs[:team]
    out_ref, left, right, gram, start, noise = refs[team:]
    diagonal_at = news_ref.shape[1] - BLK_DEV
    order = size * BS
    rhs = start.shape[0]
    mine = lax.axis_index("rows") % team
    lane = lax.broadcasted_iota(jnp.int32, (BS, LANES), 1)
    line = lax.broadcasted_iota(jnp.int32, (LANES, BS), 0)
    spots = []
    for place in range(size):
        home = info_ref[place, 0] // BLK_DEV
        member = home % team
        slot = home // team
        spots.append((member, slot))
        tile = parts[0][slot]
        for other in range(1, team):
            tile = jnp.where(member ^ mine == other, parts[other][slot], tile)
        rows = slice(place * BS, (place + 1) * BS)
        emb = tile[:BS].astype(F32)
        turned = emb.T
        left[rows, :emb_width] = tile[:BS]
        right[:emb_width, rows] = (turned * -2.0).astype(BF16)
        top, middle, low = split3(jnp.sum(emb * emb, axis=1, keepdims=True))
        extra = jnp.where(lane < 2 * 3, 1.0, 0.0)
        extra = jnp.where(lane == 2, low, extra)
        extra = jnp.where(lane == 1, middle, extra)
        left[rows, emb_width:] = jnp.where(lane == 0, top, extra).astype(BF16)
        top, middle, low = split3(jnp.sum(turned * turned, axis=0, keepdims=True))
        extra = jnp.where(line < 3, 1.0, 0.0)
        extra = jnp.where(line == 5, low, extra)
        extra = jnp.where(line == 4, middle, extra)
        right[emb_width:, rows] = jnp.where(line == 3, top, extra).astype(BF16)
        start[:, rows] = tile[BS : BS + rhs].astype(F32)
        noise[:, rows] = news_ref[home, pl.ds(diagonal_at + info_ref[place, 0] % BLK_DEV, 1), :]

    rate = math.sqrt(5.0) / (0.5 * math.sqrt(2.0 * emb_width))
    chunk = 256
    for column in range(0, order, chunk):
        columns = slice(column, column + chunk)
        distance_sq = jnp.dot(
            left[: column + chunk, :], right[:, columns], preferred_element_type=F32
        )
        distance_sq = jnp.maximum(distance_sq, 1e-12)
        distance = distance_sq * lax.rsqrt(distance_sq)
        value = (distance * (rate * rate / 3.0) + rate) * distance + 1.0
        value = (value * jnp.exp2(distance * (-rate * math.log2(math.e)))).astype(BF16)
        gram[: column + chunk, columns] = value
        for above in range(0, column, chunk):
            gram[columns, above : above + chunk] = value[above : above + chunk].T

    basis, numbers, scales = [start[...]], [], []
    for step in range(STEPS):
        vector = basis[step]
        image = jnp.dot(vector.astype(BF16), gram[...], preferred_element_type=F32)
        square = jnp.sum(vector * vector, axis=1, keepdims=True)
        scales.append(jnp.where(square > 0.0, 1.0 / square, 0.0))
        image = image + noise[...] * vector
        parts_of = [
            jnp.sum(one * image, axis=1, keepdims=True) * scale
            for one, scale in zip(basis, scales, strict=True)
        ]
        for one, part in zip(basis, parts_of, strict=True):
            image = image - part * one
        basis.append(image)
        numbers += [square] + parts_of

    spot = lax.broadcasted_iota(jnp.int32, (rhs, LANES), 1)
    table = jnp.zeros((rhs, LANES), F32)
    for index, number in enumerate(numbers):
        table = jnp.where(spot == index, number, table)
    table = jnp.concatenate([table, jnp.zeros((LANES - rhs, LANES), F32)], axis=0).T[:16]
    top, middle, low = split3(table)
    table = top + pltpu.roll(middle, rhs, 1) + pltpu.roll(low, 2 * rhs, 1)
    table = table.astype(BF16)
    for slot in range(out_ref.shape[0]):
        out_ref[slot, STEPS * rhs : (STEPS + 1) * rhs, :] = table
    for place, (member, slot) in enumerate(spots):

        @pl.when(member == mine)
        def _(place=place, slot=slot):
            for step in range(STEPS):
                out_ref[slot, step * rhs : (step + 1) * rhs, :] = basis[step + 1][
                    :, place * BS : (place + 1) * BS
                ].astype(BF16)


def combine_kernel(height, info_ref, back_ref, rhs_ref, solution_ref, residual_ref, table):
    clusters = back_ref.shape[0]
    rhs = rhs_ref.shape[0]
    for cluster in range(clusters):
        part = back_ref[cluster, STEPS * rhs : STEPS * rhs + 16, :].astype(F32)
        table[cluster] = (
            part + pltpu.roll(part, LANES - rhs, 1) + pltpu.roll(part, LANES - 2 * rhs, 1)
        )
    squares, mixing, at = [], [], 0
    for step in range(STEPS):
        squares.append(table[:, at, :])
        mixing.append([table[:, at + 1 + k, :] for k in range(step + 1)])
        at += step + 2
    one = jnp.ones_like(squares[0])
    solution, residual, direction = [], [one], [one]

    def total(values):
        return jnp.sum(functools.reduce(jnp.add, values), axis=0, keepdims=True)

    norm_now = total([squares[0]])
    for step in range(STEPS):
        image = []
        for out in range(step + 2):
            terms = [mixing[k][out] * direction[k] for k in range(out, step + 1)]
            image.append(functools.reduce(jnp.add, terms + direction[out - 1 : out]))
        step_len = norm_now / total(
            [squares[k] * direction[k] * image[k] for k in range(step + 1)]
        )
        solution = [x + step_len * p for x, p in zip(solution, direction)] + [
            step_len * direction[step]
        ]
        residual = [r - step_len * w for r, w in zip(residual, image)] + [-step_len * image[-1]]
        if step == STEPS - 1:
            break
        norm_next = total([squares[k] * residual[k] * residual[k] for k in range(step + 2)])
        ratio = norm_next / norm_now
        direction = [r + ratio * p for r, p in zip(residual, direction)] + [residual[-1]]
        norm_now = norm_next
    for index, coefficient in enumerate(solution + residual):
        table[:, index, :] = coefficient
    labels = [info_ref[height + slot, 0] for slot in range(BLK_DEV)]
    coefs = [table[label, 0:8, :] for label in labels]
    turned = jnp.concatenate(coefs + [jnp.zeros((LANES - 8 * BLK_DEV, LANES), F32)], axis=0).T
    for slot, label in enumerate(labels):
        block = slice(slot * BS, (slot + 1) * BS)
        vectors = [rhs_ref[:, block]] + [
            back_ref[label, step * rhs : (step + 1) * rhs, :].astype(F32) for step in range(STEPS)
        ]
        weights = [turned[:rhs, slot * 8 + k : slot * 8 + k + 1] for k in range(2 * STEPS + 1)]
        solution_ref[:, block] = functools.reduce(
            jnp.add, [weights[k] * vectors[k] for k in range(STEPS)]
        )
        residual_ref[:, block] = functools.reduce(
            jnp.add, [weights[STEPS + k] * vectors[k] for k in range(STEPS + 1)]
        )


def local(embeddings, noise_diag, right_side, pairs):
    devices = lax.axis_size("rows")
    emb_width = embeddings.shape[1]
    rhs, local_rows = right_side.shape
    count = pairs.shape[1]
    size = count // 2 - 1
    team = size // BLK_DEV
    clusters = devices // team
    height = max(8, size)
    slot_rows = BS + rhs
    vmem = pl.BlockSpec(memory_space=pltpu.VMEM)
    smem = pl.BlockSpec(memory_space=pltpu.SMEM)
    hbm = pl.BlockSpec(memory_space=pltpu.HBM)
    params = pltpu.CompilerParams(vmem_limit_bytes=48 * 1024 * 1024)

    news_rows = 8 * pl.cdiv(BLK_DEV + pl.cdiv(devices * BLK_DEV, LANES), 8)
    every = pl.pallas_call(
        announce_kernel,
        out_shape=jax.ShapeDtypeStruct((devices, news_rows, LANES), F32),
        in_specs=[hbm, hbm],
        out_specs=vmem,
        scratch_shapes=[
            pltpu.SMEM((2, count), jnp.int32),
            pltpu.VMEM((BLK_DEV, BS), F32),
            pltpu.SemaphoreType.DMA((2,)),
        ],
        compiler_params=params,
        name="announce",
    )(pairs, noise_diag.reshape(BLK_DEV, BS))
    every = lax.all_to_all(every, "rows", split_axis=0, concat_axis=0, tiled=True)
    packed, info = pl.pallas_call(
        functools.partial(plan_kernel, team, size),
        out_shape=(
            jax.ShapeDtypeStruct((clusters, slot_rows, LANES), BF16),
            jax.ShapeDtypeStruct((height + 8, LANES), jnp.int32),
        ),
        in_specs=[vmem] * 3,
        out_specs=(vmem, vmem),
        compiler_params=params,
        name="plan",
    )(every, embeddings, right_side)
    same = [[lead * team + member for lead in range(clusters)] for member in range(team)]
    parts = [
        lax.all_to_all(
            packed, "rows", split_axis=0, concat_axis=0, tiled=True, axis_index_groups=same
        )
    ]
    reach = 1
    while reach < team:
        parts = parts + [
            lax.ppermute(one, "rows", [(i, i ^ reach) for i in range(devices)]) for one in parts
        ]
        reach *= 2
    order = size * BS
    back = pl.pallas_call(
        functools.partial(krylov_kernel, team, size, emb_width),
        out_shape=jax.ShapeDtypeStruct((clusters, (STEPS + 1) * rhs, LANES), BF16),
        in_specs=[smem] + [vmem] * (team + 1),
        out_specs=vmem,
        scratch_shapes=[
            pltpu.VMEM((order, 2 * emb_width), BF16),
            pltpu.VMEM((2 * emb_width, order), BF16),
            pltpu.VMEM((order, order), BF16),
            pltpu.VMEM((rhs, order), F32),
            pltpu.VMEM((1, order), F32),
        ],
        compiler_params=params,
        name="krylov",
    )(info, every, *parts)
    back = lax.all_to_all(
        back, "rows", split_axis=0, concat_axis=0, tiled=True, axis_index_groups=same
    )
    return pl.pallas_call(
        functools.partial(combine_kernel, height),
        out_shape=(
            jax.ShapeDtypeStruct((rhs, local_rows), F32),
            jax.ShapeDtypeStruct((rhs, local_rows), F32),
        ),
        in_specs=[smem, vmem, vmem],
        out_specs=(vmem, vmem),
        scratch_shapes=[pltpu.VMEM((clusters, 16, LANES), F32)],
        compiler_params=params,
        name="combine",
    )(info, back, right_side)


def solution(mesh):
    in_specs = (
        P(("groups", "rows"), None),
        P(("groups", "rows")),
        P(None, ("groups", "rows")),
        P(None, ("groups", "rows")),
    )
    out_specs = (P(None, ("groups", "rows")), P(None, ("groups", "rows")))
    return jax.shard_map(local, mesh=mesh, in_specs=in_specs, out_specs=out_specs, check_vma=False)
```

```python
import functools
import math

import jax
import jax.numpy as jnp
from jax import lax
from jax.experimental import pallas as pl
from jax.experimental.pallas import tpu as pltpu
from jax.sharding import PartitionSpec as P

BS = 128
BLK_DEV = 4
STEPS = 3
LANES = 128
F32 = jnp.float32
BF16 = jnp.bfloat16


def split3(value):
    high = value.astype(BF16).astype(F32)
    rest = value - high
    middle = rest.astype(BF16).astype(F32)
    return high, middle, rest - middle


def announce_kernel(raw_ref, out_ref, *, count):
    devices, height, _ = out_ref.shape
    named_rows = pl.cdiv(devices * BLK_DEV, LANES)
    lane = lax.broadcasted_iota(jnp.int32, (2, LANES), 1).astype(F32)
    line = lax.broadcasted_iota(jnp.int32, (height, LANES), 0)
    tile = raw_ref[...]
    ids = tile[:2]
    for row in range(named_rows):
        hit = jnp.zeros((2, LANES), F32)
        for item in range(count):
            hit = jnp.where(lane + row * LANES == ids[:, item : item + 1], 1.0, hit)
        tile = jnp.where(line == row, jnp.max(hit, axis=0, keepdims=True), tile)
    for device in range(devices):
        out_ref[device] = tile


def plan_kernel(team, size, news_ref, emb_ref, rhs_ref, packed_ref, info_ref):
    devices = news_ref.shape[0]
    width = pl.cdiv(devices * BLK_DEV, LANES) * LANES
    rhs = rhs_ref.shape[0]
    me = lax.axis_index("rows")
    named = jnp.concatenate([news_ref[:, line, :] for line in range(width // LANES)], axis=1)
    named = named.astype(BF16)
    together = lax.dot_general(named, named, (((1,), (1,)), ((), ())), preferred_element_type=F32)
    together = together > 0.0
    if team > 2:
        link = together.astype(F32).astype(BF16)
        together = jnp.dot(link, link, preferred_element_type=F32) > 0.0
    link = together.astype(F32)
    members = jnp.dot(link.astype(BF16), named, preferred_element_type=F32) > 0.0
    down = lax.broadcasted_iota(jnp.int32, (devices, devices), 0).astype(F32)
    across = lax.broadcasted_iota(jnp.int32, (devices, devices), 1).astype(F32)
    far = float(devices)
    leader_down = jnp.min(jnp.where(together, across, far), axis=1, keepdims=True)
    leader_across = jnp.min(jnp.where(together, down, far), axis=0, keepdims=True)
    first = leader_across == across
    rank = jnp.sum(
        jnp.where(jnp.logical_and(first, across < leader_down), 1.0, 0.0), axis=1, keepdims=True
    )
    label = jnp.max(jnp.where(members, rank, 0.0), axis=0, keepdims=True)

    lane = lax.broadcasted_iota(jnp.int32, (1, width), 1)
    spots = []
    for slot in range(BLK_DEV):
        mine = jnp.sum(jnp.where(lane == me * BLK_DEV + slot, label, 0.0)).astype(jnp.int32)
        spots.append(mine)
        rows = slice(slot * BS, (slot + 1) * BS)
        packed_ref[mine, 0:BS, :] = emb_ref[rows, :]
        packed_ref[mine, BS : BS + rhs, :] = rhs_ref[:, rows].astype(BF16)

    height = info_ref.shape[0] - 8
    hit = jnp.where(label == (me // team).astype(F32), 1.0, 0.0)
    hit = jnp.broadcast_to(hit, (height, width))
    upper = lax.broadcasted_iota(jnp.int32, (width, width), 0) <= lax.broadcasted_iota(
        jnp.int32, (width, width), 1
    )
    before = jnp.dot(
        hit.astype(BF16), upper.astype(F32).astype(BF16), preferred_element_type=F32
    )
    place = lax.broadcasted_iota(jnp.int32, (height, width), 0).astype(F32) + 1.0
    ids = lax.broadcasted_iota(jnp.int32, (height, width), 1).astype(F32)
    chosen = jnp.where(jnp.logical_and(hit > 0.0, before == place), ids, 0.0)
    order = jnp.sum(chosen, axis=1, keepdims=True).astype(jnp.int32)
    info_ref[0:height, :] = jnp.broadcast_to(order, (height, LANES))
    line = lax.broadcasted_iota(jnp.int32, (8, LANES), 0)
    own = jnp.zeros((8, LANES), jnp.int32)
    for slot in range(BLK_DEV):
        own = jnp.where(line == slot, spots[slot], own)
    info_ref[height : height + 8, :] = own


def krylov_kernel(team, size, emb_width, info_ref, news_ref, *refs):
    parts = refs[:team]
    out_ref, left, right, gram, start, noise = refs[team:]
    diagonal_at = news_ref.shape[1] - BLK_DEV
    order = size * BS
    rhs = start.shape[0]
    mine = lax.axis_index("rows") % team
    lane = lax.broadcasted_iota(jnp.int32, (BS, LANES), 1)
    line = lax.broadcasted_iota(jnp.int32, (LANES, BS), 0)
    spots = []
    for place in range(size):
        block = jnp.max(info_ref[place : place + 1, :])
        home = block // BLK_DEV
        member = home % team
        slot = home // team
        spots.append((member, slot))
        tile = parts[0][slot]
        for other in range(1, team):
            tile = jnp.where(member ^ mine == other, parts[other][slot], tile)
        rows = slice(place * BS, (place + 1) * BS)
        emb = tile[:BS].astype(F32)
        turned = emb.T
        left[rows, :emb_width] = tile[:BS]
        right[:emb_width, rows] = (turned * -2.0).astype(BF16)
        top, middle, low = split3(jnp.sum(emb * emb, axis=1, keepdims=True))
        extra = jnp.where(lane < 2 * 3, 1.0, 0.0)
        extra = jnp.where(lane == 2, low, extra)
        extra = jnp.where(lane == 1, middle, extra)
        left[rows, emb_width:] = jnp.where(lane == 0, top, extra).astype(BF16)
        top, middle, low = split3(jnp.sum(turned * turned, axis=0, keepdims=True))
        extra = jnp.where(line < 3, 1.0, 0.0)
        extra = jnp.where(line == 5, low, extra)
        extra = jnp.where(line == 4, middle, extra)
        right[emb_width:, rows] = jnp.where(line == 3, top, extra).astype(BF16)
        start[:, rows] = tile[BS : BS + rhs].astype(F32)
        noise[:, rows] = news_ref[home, pl.ds(diagonal_at + block % BLK_DEV, 1), :]

    rate = math.sqrt(5.0) / (0.5 * math.sqrt(2.0 * emb_width))
    chunk = 256
    for column in range(0, order, chunk):
        columns = slice(column, column + chunk)
        distance_sq = jnp.dot(
            left[: column + chunk, :], right[:, columns], preferred_element_type=F32
        )
        distance_sq = jnp.maximum(distance_sq, 1e-12)
        distance = distance_sq * lax.rsqrt(distance_sq)
        value = (distance * (rate * rate / 3.0) + rate) * distance + 1.0
        value = (value * jnp.exp2(distance * (-rate * math.log2(math.e)))).astype(BF16)
        gram[: column + chunk, columns] = value
        for above in range(0, column, chunk):
            gram[columns, above : above + chunk] = value[above : above + chunk].T

    basis, numbers, scales = [start[...]], [], []
    for step in range(STEPS):
        vector = basis[step]
        image = jnp.dot(vector.astype(BF16), gram[...], preferred_element_type=F32)
        square = jnp.sum(vector * vector, axis=1, keepdims=True)
        scales.append(jnp.where(square > 0.0, 1.0 / square, 0.0))
        image = image + noise[...] * vector
        parts_of = [
            jnp.sum(one * image, axis=1, keepdims=True) * scale
            for one, scale in zip(basis, scales, strict=True)
        ]
        for one, part in zip(basis, parts_of, strict=True):
            image = image - part * one
        basis.append(image)
        numbers += [square] + parts_of

    spot = lax.broadcasted_iota(jnp.int32, (rhs, LANES), 1)
    table = jnp.zeros((rhs, LANES), F32)
    for index, number in enumerate(numbers):
        table = jnp.where(spot == index, number, table)
    table = jnp.concatenate([table, jnp.zeros((LANES - rhs, LANES), F32)], axis=0).T[:16]
    top, middle, low = split3(table)
    table = top + pltpu.roll(middle, rhs, 1) + pltpu.roll(low, 2 * rhs, 1)
    table = table.astype(BF16)
    for slot in range(out_ref.shape[0]):
        out_ref[slot, STEPS * rhs : (STEPS + 1) * rhs, :] = table
    for place, (member, slot) in enumerate(spots):

        @pl.when(member == mine)
        def _(place=place, slot=slot):
            for step in range(STEPS):
                out_ref[slot, step * rhs : (step + 1) * rhs, :] = basis[step + 1][
                    :, place * BS : (place + 1) * BS
                ].astype(BF16)


def combine_kernel(height, info_ref, back_ref, rhs_ref, solution_ref, residual_ref, table):
    clusters = back_ref.shape[0]
    rhs = rhs_ref.shape[0]
    for cluster in range(clusters):
        part = back_ref[cluster, STEPS * rhs : STEPS * rhs + 16, :].astype(F32)
        table[cluster] = (
            part + pltpu.roll(part, LANES - rhs, 1) + pltpu.roll(part, LANES - 2 * rhs, 1)
        )
    squares, mixing, at = [], [], 0
    for step in range(STEPS):
        squares.append(table[:, at, :])
        mixing.append([table[:, at + 1 + k, :] for k in range(step + 1)])
        at += step + 2
    one = jnp.ones_like(squares[0])
    solution, residual, direction = [], [one], [one]

    def total(values):
        return jnp.sum(functools.reduce(jnp.add, values), axis=0, keepdims=True)

    norm_now = total([squares[0]])
    for step in range(STEPS):
        image = []
        for out in range(step + 2):
            terms = [mixing[k][out] * direction[k] for k in range(out, step + 1)]
            image.append(functools.reduce(jnp.add, terms + direction[out - 1 : out]))
        step_len = norm_now / total(
            [squares[k] * direction[k] * image[k] for k in range(step + 1)]
        )
        solution = [x + step_len * p for x, p in zip(solution, direction)] + [
            step_len * direction[step]
        ]
        residual = [r - step_len * w for r, w in zip(residual, image)] + [-step_len * image[-1]]
        if step == STEPS - 1:
            break
        norm_next = total([squares[k] * residual[k] * residual[k] for k in range(step + 2)])
        ratio = norm_next / norm_now
        direction = [r + ratio * p for r, p in zip(residual, direction)] + [residual[-1]]
        norm_now = norm_next
    for index, coefficient in enumerate(solution + residual):
        table[:, index, :] = coefficient
    labels = [
        jnp.max(info_ref[height + slot : height + slot + 1, :]) for slot in range(BLK_DEV)
    ]
    coefs = [table[label, 0:8, :] for label in labels]
    turned = jnp.concatenate(coefs + [jnp.zeros((LANES - 8 * BLK_DEV, LANES), F32)], axis=0).T
    for slot, label in enumerate(labels):
        block = slice(slot * BS, (slot + 1) * BS)
        vectors = [rhs_ref[:, block]] + [
            back_ref[label, step * rhs : (step + 1) * rhs, :].astype(F32) for step in range(STEPS)
        ]
        weights = [turned[:rhs, slot * 8 + k : slot * 8 + k + 1] for k in range(2 * STEPS + 1)]
        solution_ref[:, block] = functools.reduce(
            jnp.add, [weights[k] * vectors[k] for k in range(STEPS)]
        )
        residual_ref[:, block] = functools.reduce(
            jnp.add, [weights[STEPS + k] * vectors[k] for k in range(STEPS + 1)]
        )


def local(embeddings, noise_diag, right_side, pairs):
    devices = lax.axis_size("rows")
    emb_width = embeddings.shape[1]
    rhs, local_rows = right_side.shape
    count = pairs.shape[1]
    size = count // 2 - 1
    team = size // BLK_DEV
    clusters = devices // team
    height = max(8, size)
    slot_rows = BS + rhs
    vmem = pl.BlockSpec(memory_space=pltpu.VMEM)
    anywhere = pl.BlockSpec(memory_space=pl.ANY)
    params = pltpu.CompilerParams(vmem_limit_bytes=48 * 1024 * 1024)

    news_rows = 8 * pl.cdiv(BLK_DEV + pl.cdiv(devices * BLK_DEV, LANES), 8)
    raw = jnp.concatenate(
        [
            jnp.pad(pairs.astype(F32), ((0, news_rows - BLK_DEV - 2), (0, LANES - count))),
            noise_diag.reshape(BLK_DEV, BS),
        ]
    )
    every = pl.pallas_call(
        functools.partial(announce_kernel, count=count),
        out_shape=jax.ShapeDtypeStruct((devices, news_rows, LANES), F32),
        in_specs=[vmem],
        out_specs=vmem,
        compiler_params=params,
        name="announce",
    )(raw)
    every = lax.all_to_all(every, "rows", split_axis=0, concat_axis=0, tiled=True)
    packed, info = pl.pallas_call(
        functools.partial(plan_kernel, team, size),
        out_shape=(
            jax.ShapeDtypeStruct((clusters, slot_rows, LANES), BF16),
            jax.ShapeDtypeStruct((height + 8, LANES), jnp.int32),
        ),
        in_specs=[vmem] * 3,
        out_specs=(vmem, vmem),
        compiler_params=params,
        name="plan",
    )(every, embeddings, right_side)
    same = [[lead * team + member for lead in range(clusters)] for member in range(team)]
    parts = [
        lax.all_to_all(
            packed, "rows", split_axis=0, concat_axis=0, tiled=True, axis_index_groups=same
        )
    ]
    reach = 1
    while reach < team:
        parts = parts + [
            lax.ppermute(one, "rows", [(i, i ^ reach) for i in range(devices)]) for one in parts
        ]
        reach *= 2
    order = size * BS
    back = pl.pallas_call(
        functools.partial(krylov_kernel, team, size, emb_width),
        out_shape=jax.ShapeDtypeStruct((clusters, (STEPS + 1) * rhs, LANES), BF16),
        in_specs=[vmem] * (team + 2),
        out_specs=vmem,
        scratch_shapes=[
            pltpu.VMEM((order, 2 * emb_width), BF16),
            pltpu.VMEM((2 * emb_width, order), BF16),
            pltpu.VMEM((order, order), BF16),
            pltpu.VMEM((rhs, order), F32),
            pltpu.VMEM((1, order), F32),
        ],
        compiler_params=params,
        name="krylov",
    )(info, every, *parts)
    back = lax.all_to_all(
        back, "rows", split_axis=0, concat_axis=0, tiled=True, axis_index_groups=same
    )
    return pl.pallas_call(
        functools.partial(combine_kernel, height),
        out_shape=(
            jax.ShapeDtypeStruct((rhs, local_rows), F32),
            jax.ShapeDtypeStruct((rhs, local_rows), F32),
        ),
        in_specs=[vmem] * 3,
        out_specs=(vmem, vmem),
        scratch_shapes=[pltpu.VMEM((clusters, 16, LANES), F32)],
        compiler_params=params,
        name="combine",
    )(info, back, right_side)


def solution(mesh):
    in_specs = (
        P(("groups", "rows"), None),
        P(("groups", "rows")),
        P(None, ("groups", "rows")),
        P(None, ("groups", "rows")),
    )
    out_specs = (P(None, ("groups", "rows")), P(None, ("groups", "rows")))
    return jax.shard_map(local, mesh=mesh, in_specs=in_specs, out_specs=out_specs, check_vma=False)
```

```python
import functools
import math

import jax
import jax.numpy as jnp
from jax import lax
from jax.experimental import pallas as pl
from jax.experimental.pallas import tpu as pltpu
from jax.sharding import PartitionSpec as P

BS = 128
BLK_DEV = 4
STEPS = 3
LANES = 128
F32 = jnp.float32
BF16 = jnp.bfloat16


def split3(value):
    high = value.astype(BF16).astype(F32)
    rest = value - high
    middle = rest.astype(BF16).astype(F32)
    return high, middle, rest - middle


def announce_kernel(
    pairs_hbm, noise_hbm, emb_hbm, rhs_hbm, out_ref, own_ref, pairs_ref, noise_ref, rhs_ref, arrived
):
    rhs = rhs_hbm.shape[0]
    moves = [(pairs_hbm, pairs_ref), (noise_hbm, noise_ref), (rhs_hbm, rhs_ref)]
    for slot in range(BLK_DEV):
        moves.append((emb_hbm.at[slot * BS : (slot + 1) * BS, :], own_ref.at[slot, :BS, :]))
    fetches = [
        pltpu.make_async_copy(source, target, arrived.at[index])
        for index, (source, target) in enumerate(moves)
    ]
    for fetch in fetches:
        fetch.start()
    devices, height, _ = out_ref.shape
    named_rows = pl.cdiv(devices * BLK_DEV, LANES)
    lane = lax.broadcasted_iota(jnp.int32, (2, LANES), 1)
    line = lax.broadcasted_iota(jnp.int32, (height, LANES), 0)
    tile = jnp.zeros((height, LANES), F32)
    fetches[0].wait()
    ids = pairs_ref[...]
    for row in range(named_rows):
        hit = jnp.zeros((2, LANES), F32)
        for item in range(ids.shape[1]):
            hit = jnp.where(lane + row * LANES == ids[:, item : item + 1], 1.0, hit)
        tile = jnp.where(line == row, jnp.max(hit, axis=0, keepdims=True), tile)
    fetches[1].wait()
    for slot in range(BLK_DEV):
        tile = jnp.where(line == height - BLK_DEV + slot, noise_ref[slot : slot + 1, :], tile)
    for device in range(devices):
        out_ref[device] = tile
    fetches[2].wait()
    for slot in range(BLK_DEV):
        own_ref[slot, BS : BS + rhs, :] = rhs_ref[:, slot * BS : (slot + 1) * BS].astype(BF16)
    for fetch in fetches[3:]:
        fetch.wait()


def plan_kernel(team, news_ref, own_ref, far_ref, *outs):
    *packed_refs, label_ref = outs
    devices = news_ref.shape[0]
    width = pl.cdiv(devices * BLK_DEV, LANES) * LANES
    me = lax.axis_index("rows")
    named = jnp.concatenate([news_ref[:, line, :] for line in range(width // LANES)], axis=1)
    named = named.astype(BF16)
    together = lax.dot_general(named, named, (((1,), (1,)), ((), ())), preferred_element_type=F32)
    together = together > 0.0
    if team > 2:
        link = together.astype(F32).astype(BF16)
        together = jnp.dot(link, link, preferred_element_type=F32) > 0.0
    link = together.astype(F32)
    members = jnp.dot(link.astype(BF16), named, preferred_element_type=F32) > 0.0
    down = lax.broadcasted_iota(jnp.int32, (devices, devices), 0).astype(F32)
    across = lax.broadcasted_iota(jnp.int32, (devices, devices), 1).astype(F32)
    far = float(devices)
    leader_down = jnp.min(jnp.where(together, across, far), axis=1, keepdims=True)
    leader_across = jnp.min(jnp.where(together, down, far), axis=0, keepdims=True)
    first = leader_across == across
    rank = jnp.sum(
        jnp.where(jnp.logical_and(first, across < leader_down), 1.0, 0.0), axis=1, keepdims=True
    )
    label = jnp.max(jnp.where(members, rank, 0.0), axis=0, keepdims=True)

    label_ref[...] = jnp.broadcast_to(label, label_ref.shape)
    lane = lax.broadcasted_iota(jnp.int32, (1, width), 1)

    def labels_of(device):
        return [
            jnp.sum(jnp.where(lane == device * BLK_DEV + slot, label, 0.0)).astype(jnp.int32)
            for slot in range(BLK_DEV)
        ]

    far = me ^ (devices // 2)
    sources = [(own_ref, labels_of(me)), (far_ref, labels_of(far))]
    for mask, packed_ref in enumerate(packed_refs):
        target = (me // team) ^ mask
        for side, (blocks, labels) in enumerate(sources):
            packed_ref[side] = blocks[sum(jnp.where(labels[k] == target, k, 0) for k in range(1, BLK_DEV))]


def places_kernel(team, size, label_ref, news_ref, place_ref, noise_ref):
    devices, news_rows, _ = news_ref.shape
    height, width = label_ref.shape
    me = lax.axis_index("rows")
    hit = jnp.where(label_ref[...] == (me // team).astype(F32), 1.0, 0.0)
    down = lax.broadcasted_iota(jnp.int32, (width, width), 0)
    across = lax.broadcasted_iota(jnp.int32, (width, width), 1)
    upper = jnp.where(down <= across, 1.0, 0.0).astype(BF16)
    before = jnp.dot(hit.astype(BF16), upper, preferred_element_type=F32)
    home = lax.broadcasted_iota(jnp.int32, (width, LANES), 0) // BLK_DEV
    relative = lax.broadcasted_iota(jnp.int32, (width, LANES), 1)
    chosen = jnp.where((home ^ me) == relative, 1.0, 0.0).astype(BF16)
    offset = (hit * (before - 1.0 - size)).astype(BF16)
    place = jnp.dot(offset, chosen, preferred_element_type=F32)[:1] + float(size)
    column = lax.broadcasted_iota(jnp.int32, place_ref.shape, 1)
    line = lax.broadcasted_iota(jnp.int32, place_ref.shape, 0)
    weight = jnp.where(column % 4 == 0, 1.0, jnp.where(column % 4 == 1, 32.0, 1024.0))
    weight = jnp.where(column % 4 == 3, 32768.0, weight)
    place_ref[...] = jnp.where(column // 4 == line, place * weight, 0.0)
    block_id = lax.broadcasted_iota(jnp.int32, (1, width), 1).astype(F32)
    for spot in range(size):
        here = jnp.logical_and(hit[:1] > 0.0, before[:1] == spot + 1.0)
        block = jnp.sum(jnp.where(here, block_id, 0.0)).astype(jnp.int32)
        row = news_rows - BLK_DEV + block % BLK_DEV
        noise_ref[:, spot * BS : (spot + 1) * BS] = news_ref[block // BLK_DEV, pl.ds(row, 1), :]


def merge_kernel(place_ref, *refs):
    *parts, out_ref = refs
    for mask, part in enumerate(parts):
        out_ref[2 * mask : 2 * mask + 2] = part[...]


def krylov_kernel(team, size, emb_width, place_ref, noise, *refs):
    *parts, out_ref, blocks, left, right, gram, start, vectors = refs
    order = size * BS
    rhs = start.shape[0]
    clusters = parts[0].shape[0]
    devices = team * clusters
    packed = [
        jnp.sum(place_ref[group : group + 1, :]).astype(jnp.int32) for group in range(devices // 4)
    ]
    places = [(packed[index // 4] >> (5 * (index % 4))) & 31 for index in range(devices)]
    for index in range(devices):
        member, chip = index % team, index // team
        mask, side = chip % (clusters // 2), chip // (clusters // 2)
        blocks[places[index]] = parts[member][2 * mask + side]
    lane = lax.broadcasted_iota(jnp.int32, (BS, LANES), 1)
    line = lax.broadcasted_iota(jnp.int32, (LANES, BS), 0)
    for place in range(size):
        tile = blocks[place]
        rows = slice(place * BS, (place + 1) * BS)
        emb = tile[:BS].astype(F32)
        turned = emb.T
        left[rows, :emb_width] = tile[:BS]
        right[:emb_width, rows] = (turned * -2.0).astype(BF16)
        top, middle, low = split3(jnp.sum(emb * emb, axis=1, keepdims=True))
        extra = jnp.where(lane < 2 * 3, 1.0, 0.0)
        extra = jnp.where(lane == 2, low, extra)
        extra = jnp.where(lane == 1, middle, extra)
        left[rows, emb_width:] = jnp.where(lane == 0, top, extra).astype(BF16)
        top, middle, low = split3(jnp.sum(turned * turned, axis=0, keepdims=True))
        extra = jnp.where(line < 3, 1.0, 0.0)
        extra = jnp.where(line == 5, low, extra)
        extra = jnp.where(line == 4, middle, extra)
        right[emb_width:, rows] = jnp.where(line == 3, top, extra).astype(BF16)
        start[:, rows] = tile[BS : BS + rhs].astype(F32)

    rate = math.sqrt(5.0) / (0.5 * math.sqrt(2.0 * emb_width))
    chunk = 256
    for column in range(0, order, chunk):
        columns = slice(column, column + chunk)
        distance_sq = jnp.dot(
            left[: column + chunk, :], right[:, columns], preferred_element_type=F32
        )
        distance_sq = jnp.maximum(distance_sq, 1e-12)
        distance = distance_sq * lax.rsqrt(distance_sq)
        value = (distance * (rate * rate / 3.0) + rate) * distance + 1.0
        value = (value * jnp.exp2(distance * (-rate * math.log2(math.e)))).astype(BF16)
        gram[: column + chunk, columns] = value
        for above in range(0, column, chunk):
            gram[columns, above : above + chunk] = value[above : above + chunk].T

    basis, numbers, scales = [start[...]], [], []
    for step in range(STEPS):
        vector = basis[step]
        image = jnp.dot(vector.astype(BF16), gram[...], preferred_element_type=F32)
        square = jnp.sum(vector * vector, axis=1, keepdims=True)
        scales.append(jnp.where(square > 0.0, 1.0 / square, 0.0))
        image = image + noise[...] * vector
        parts_of = [
            jnp.sum(one * image, axis=1, keepdims=True) * scale
            for one, scale in zip(basis, scales, strict=True)
        ]
        for one, part in zip(basis, parts_of, strict=True):
            image = image - part * one
        basis.append(image)
        vectors[step * rhs : (step + 1) * rhs, :order] = image.astype(BF16)
        numbers += [square] + parts_of

    spot = lax.broadcasted_iota(jnp.int32, (rhs, LANES), 1)
    table = jnp.zeros((rhs, LANES), F32)
    for index, number in enumerate(numbers):
        table = jnp.where(spot == index, number, table)
    table = jnp.concatenate([table, jnp.zeros((LANES - rhs, LANES), F32)], axis=0).T[:16]
    top, middle, low = split3(table)
    table = top + pltpu.roll(middle, rhs, 1) + pltpu.roll(low, 2 * rhs, 1)
    table = table.astype(BF16)
    for slot in range(out_ref.shape[0]):
        out_ref[slot, STEPS * rhs : (STEPS + 1) * rhs, :] = table
    chip = lax.axis_index("rows") // team
    for other in range(devices // team):
        at = pl.ds(pl.multiple_of(places[other * team] * BS, BS), BS)
        out_ref[chip ^ other, : STEPS * rhs, :] = vectors[:, at]


def combine_kernel(label_ref, back_ref, rhs_ref, solution_ref, residual_ref, table):
    clusters = back_ref.shape[0]
    rhs = rhs_ref.shape[0]
    for cluster in range(clusters):
        part = back_ref[cluster, STEPS * rhs : STEPS * rhs + 16, :].astype(F32)
        table[cluster] = (
            part + pltpu.roll(part, LANES - rhs, 1) + pltpu.roll(part, LANES - 2 * rhs, 1)
        )
    squares, mixing, at = [], [], 0
    for step in range(STEPS):
        squares.append(table[:, at, :])
        mixing.append([table[:, at + 1 + k, :] for k in range(step + 1)])
        at += step + 2
    one = jnp.ones_like(squares[0])
    solution, residual, direction = [], [one], [one]

    def total(values):
        return jnp.sum(functools.reduce(jnp.add, values), axis=0, keepdims=True)

    norm_now = total([squares[0]])
    for step in range(STEPS):
        image = []
        for out in range(step + 2):
            terms = [mixing[k][out] * direction[k] for k in range(out, step + 1)]
            image.append(functools.reduce(jnp.add, terms + direction[out - 1 : out]))
        step_len = norm_now / total(
            [squares[k] * direction[k] * image[k] for k in range(step + 1)]
        )
        solution = [x + step_len * p for x, p in zip(solution, direction)] + [
            step_len * direction[step]
        ]
        residual = [r - step_len * w for r, w in zip(residual, image)] + [-step_len * image[-1]]
        if step == STEPS - 1:
            break
        norm_next = total([squares[k] * residual[k] * residual[k] for k in range(step + 2)])
        ratio = norm_next / norm_now
        direction = [r + ratio * p for r, p in zip(residual, direction)] + [residual[-1]]
        norm_now = norm_next
    for index, coefficient in enumerate(solution + residual):
        table[:, index, :] = coefficient
    lane = lax.broadcasted_iota(jnp.int32, (1, label_ref.shape[1]), 1) - BLK_DEV * lax.axis_index("rows")
    labels = [
        jnp.sum(jnp.where(lane == slot, label_ref[:1, :], 0.0)).astype(jnp.int32)
        for slot in range(BLK_DEV)
    ]
    coefs = [table[label, 0:8, :] for label in labels]
    turned = jnp.concatenate(coefs + [jnp.zeros((LANES - 8 * BLK_DEV, LANES), F32)], axis=0).T
    for slot, label in enumerate(labels):
        block = slice(slot * BS, (slot + 1) * BS)
        vectors = [rhs_ref[:, block]] + [
            back_ref[label, step * rhs : (step + 1) * rhs, :].astype(F32) for step in range(STEPS)
        ]
        weights = [turned[:rhs, slot * 8 + k : slot * 8 + k + 1] for k in range(2 * STEPS + 1)]
        solution_ref[:, block] = functools.reduce(
            jnp.add, [weights[k] * vectors[k] for k in range(STEPS)]
        )
        residual_ref[:, block] = functools.reduce(
            jnp.add, [weights[STEPS + k] * vectors[k] for k in range(STEPS + 1)]
        )


def local(embeddings, noise_diag, right_side, pairs):
    devices = lax.axis_size("rows")
    emb_width = embeddings.shape[1]
    rhs, local_rows = right_side.shape
    count = pairs.shape[1]
    size = count // 2 - 1
    team = size // BLK_DEV
    clusters = devices // team
    order = size * BS
    width = pl.cdiv(devices * BLK_DEV, LANES) * LANES
    news_rows = 8 * pl.cdiv(BLK_DEV + width // LANES, 8)
    params = pltpu.CompilerParams(vmem_limit_bytes=48 * 1024 * 1024)

    def call(kernel, name, out_shape, args, scratch=(), cost=None, space=pltpu.VMEM):
        vmem = pl.BlockSpec(memory_space=pltpu.VMEM)
        return pl.pallas_call(
            kernel,
            out_shape=out_shape,
            in_specs=[pl.BlockSpec(memory_space=space)] * len(args),
            out_specs=jax.tree.map(lambda _: vmem, out_shape),
            scratch_shapes=scratch,
            compiler_params=params,
            cost_estimate=cost,
            name=name,
        )(*args)

    def swap(value, distance):
        return lax.ppermute(value, "rows", [(i, i ^ distance) for i in range(devices)])

    sources = [pairs, noise_diag.reshape(BLK_DEV, BS), embeddings, right_side]
    every, own = call(
        announce_kernel,
        "announce",
        (
            jax.ShapeDtypeStruct((devices, news_rows, LANES), F32),
            jax.ShapeDtypeStruct((BLK_DEV, BS + rhs, LANES), BF16),
        ),
        [pltpu.with_memory_space_constraint(one, pltpu.HBM) for one in sources],
        scratch=[
            pltpu.VMEM((2, count), jnp.int32),
            pltpu.VMEM((BLK_DEV, BS), F32),
            pltpu.VMEM((rhs, local_rows), F32),
            pltpu.SemaphoreType.DMA((3 + BLK_DEV,)),
        ],
        space=pltpu.HBM,
    )
    far = swap(own, devices // 2)
    every = lax.all_to_all(every, "rows", split_axis=0, concat_axis=0, tiled=True)
    every, far = lax.optimization_barrier((every, far))
    pair = jax.ShapeDtypeStruct((2, BS + rhs, LANES), BF16)
    *packed, label = call(
        functools.partial(plan_kernel, team),
        "plan",
        [pair] * (clusters // 2) + [jax.ShapeDtypeStruct((8, width), F32)],
        [every, own, far],
    )
    packed = [one if mask == 0 else swap(one, team * mask) for mask, one in enumerate(packed)]
    place, noise = call(
        functools.partial(places_kernel, team, size),
        "places",
        (
            jax.ShapeDtypeStruct((max(8, devices // 4), LANES), F32),
            jax.ShapeDtypeStruct((1, order), F32),
        ),
        [label, every],
        cost=pl.CostEstimate(flops=10**6, bytes_accessed=10**6, transcendentals=0),
    )
    parts = [
        call(
            merge_kernel,
            "merge",
            jax.ShapeDtypeStruct((clusters, BS + rhs, LANES), BF16),
            [place, *packed],
        )
    ]
    reach = 1
    while reach < team:
        parts = parts + [swap(one, reach) for one in parts]
        reach *= 2
    back = call(
        functools.partial(krylov_kernel, team, size, emb_width),
        "krylov",
        jax.ShapeDtypeStruct((clusters, (STEPS + 1) * rhs, LANES), BF16),
        [place, noise, *parts],
        scratch=[
            pltpu.VMEM((size + 1, BS + rhs, LANES), BF16),
            pltpu.VMEM((order, 2 * emb_width), BF16),
            pltpu.VMEM((2 * emb_width, order), BF16),
            pltpu.VMEM((order, order), BF16),
            pltpu.VMEM((rhs, order), F32),
            pltpu.VMEM((STEPS * rhs, order + BS), BF16),
        ],
    )
    same = [[lead * team + member for lead in range(clusters)] for member in range(team)]
    back = lax.all_to_all(
        back, "rows", split_axis=0, concat_axis=0, tiled=True, axis_index_groups=same
    )
    out = jax.ShapeDtypeStruct((rhs, local_rows), F32)
    return call(
        combine_kernel,
        "combine",
        (out, out),
        [label, back, right_side],
        scratch=[pltpu.VMEM((clusters, 16, LANES), F32)],
    )


def solution(mesh):
    in_specs = (
        P(("groups", "rows"), None),
        P(("groups", "rows")),
        P(None, ("groups", "rows")),
        P(None, ("groups", "rows")),
    )
    out_specs = (P(None, ("groups", "rows")), P(None, ("groups", "rows")))
    return jax.shard_map(local, mesh=mesh, in_specs=in_specs, out_specs=out_specs, check_vma=False)
```

```python
import functools
import math

import jax
import jax.numpy as jnp
from jax import lax
from jax.experimental import pallas as pl
from jax.experimental.pallas import tpu as pltpu
from jax.sharding import PartitionSpec as P

BS = 128
BLK_DEV = 4
STEPS = 3
LANES = 128
F32 = jnp.float32
BF16 = jnp.bfloat16


def split3(value):
    high = value.astype(BF16).astype(F32)
    rest = value - high
    middle = rest.astype(BF16).astype(F32)
    return high, middle, rest - middle


def labels_of(label, device):
    slot = lax.broadcasted_iota(jnp.int32, label.shape, 1) - device * BLK_DEV
    weight = jnp.where(slot == 0, 1.0, 0.0)
    for other in range(1, BLK_DEV):
        weight = jnp.where(slot == other, 32.0**other, weight)
    packed = jnp.sum(label * weight).astype(jnp.int32)
    return [(packed >> (5 * other)) & 31 for other in range(BLK_DEV)]


def announce_kernel(
    pairs_hbm, noise_hbm, emb_hbm, rhs_hbm, out_ref, own_ref, pairs_ref, noise_ref, rhs_ref, arrived
):
    rhs = rhs_hbm.shape[0]
    moves = [(pairs_hbm, pairs_ref), (noise_hbm, noise_ref), (rhs_hbm, rhs_ref)]
    for slot in range(BLK_DEV):
        moves.append((emb_hbm.at[slot * BS : (slot + 1) * BS, :], own_ref.at[slot, :BS, :]))
    fetches = [
        pltpu.make_async_copy(source, target, arrived.at[index])
        for index, (source, target) in enumerate(moves)
    ]
    for fetch in fetches:
        fetch.start()
    devices, height, _ = out_ref.shape
    lane = lax.broadcasted_iota(jnp.int32, (2, LANES), 1)
    line = lax.broadcasted_iota(jnp.int32, (height, LANES), 0)
    sign = jnp.ones((height, LANES), F32)
    fetches[0].wait()
    ids = pairs_ref[...]
    for row in range(pl.cdiv(devices * BLK_DEV, LANES)):
        hit = jnp.zeros((2, LANES), F32)
        for item in range(ids.shape[1]):
            hit = jnp.where(lane + row * LANES == ids[:, item : item + 1], 1.0, hit)
        named = jnp.max(hit, axis=0, keepdims=True)
        sign = jnp.where(jnp.logical_and(line == row, named > 0.0), -1.0, sign)
    fetches[1].wait()
    tile = sign * noise_ref[...]
    for device in range(devices):
        out_ref[device] = tile
    fetches[2].wait()
    for slot in range(BLK_DEV):
        own_ref[slot, BS : BS + rhs, :] = rhs_ref[:, slot * BS : (slot + 1) * BS].astype(BF16)
    for fetch in fetches[3:]:
        fetch.wait()


def plan_kernel(team, news_ref, own_ref, far_ref, *outs):
    *packed_refs, label_ref = outs
    devices = news_ref.shape[0]
    width = pl.cdiv(devices * BLK_DEV, LANES) * LANES
    me = lax.axis_index("rows")
    named = jnp.concatenate([news_ref[:, line, :] for line in range(width // LANES)], axis=1)
    named = jnp.where(named < 0.0, 1.0, 0.0)
    flags = named.astype(BF16)
    together = lax.dot_general(flags, flags, (((1,), (1,)), ((), ())), preferred_element_type=F32)
    together = together > 0.0
    if team > 2:
        link = together.astype(F32).astype(BF16)
        together = jnp.dot(link, link, preferred_element_type=F32) > 0.0
    down = lax.broadcasted_iota(jnp.int32, (devices, devices), 0).astype(F32)
    across = lax.broadcasted_iota(jnp.int32, (devices, devices), 1).astype(F32)
    far = float(devices)
    leader_down = jnp.min(jnp.where(together, across, far), axis=1, keepdims=True)
    leader_across = jnp.min(jnp.where(together, down, far), axis=0, keepdims=True)
    first = leader_across == across
    rank = jnp.sum(
        jnp.where(jnp.logical_and(first, across < leader_down), 1.0, 0.0), axis=1, keepdims=True
    )
    label = jnp.max(named * rank, axis=0, keepdims=True)

    label_ref[...] = jnp.broadcast_to(label, label_ref.shape)
    far = me ^ (devices // 2)
    sources = [(own_ref, labels_of(label, me)), (far_ref, labels_of(label, far))]
    for mask, packed_ref in enumerate(packed_refs):
        target = (me // team) ^ mask
        for side, (blocks, labels) in enumerate(sources):
            packed_ref[side] = blocks[sum(jnp.where(labels[k] == target, k, 0) for k in range(1, BLK_DEV))]


def places_kernel(team, size, label_ref, news_ref, place_ref, noise_ref):
    devices = news_ref.shape[0]
    height, width = label_ref.shape
    me = lax.axis_index("rows")
    hit = jnp.where(label_ref[...] == (me // team).astype(F32), 1.0, 0.0)
    down = lax.broadcasted_iota(jnp.int32, (width, width), 0)
    across = lax.broadcasted_iota(jnp.int32, (width, width), 1)
    upper = jnp.where(down <= across, 1.0, 0.0).astype(BF16)
    before = jnp.dot(hit.astype(BF16), upper, preferred_element_type=F32)
    home = lax.broadcasted_iota(jnp.int32, (width, LANES), 0) // BLK_DEV
    relative = lax.broadcasted_iota(jnp.int32, (width, LANES), 1)
    chosen = jnp.where((home ^ me) == relative, 1.0, 0.0).astype(BF16)
    offset = (hit * (before - 1.0 - size)).astype(BF16)
    place = jnp.dot(offset, chosen, preferred_element_type=F32)[:1] + float(size)
    column = lax.broadcasted_iota(jnp.int32, place_ref.shape, 1)
    line = lax.broadcasted_iota(jnp.int32, place_ref.shape, 0)
    weight = jnp.where(column % 4 == 0, 1.0, jnp.where(column % 4 == 1, 32.0, 1024.0))
    weight = jnp.where(column % 4 == 3, 32768.0, weight)
    place_ref[...] = jnp.where(column // 4 == line, place * weight, 0.0)
    block_id = lax.broadcasted_iota(jnp.int32, (1, width), 1).astype(F32)
    for spot in range(size):
        here = jnp.logical_and(hit[:1] > 0.0, before[:1] == spot + 1.0)
        block = jnp.sum(jnp.where(here, block_id, 0.0)).astype(jnp.int32)
        noise_ref[:, spot * BS : (spot + 1) * BS] = jnp.abs(
            news_ref[block // BLK_DEV, pl.ds(block % BLK_DEV, 1), :]
        )


def merge_kernel(place_ref, *refs):
    *parts, out_ref = refs
    for mask, part in enumerate(parts):
        out_ref[2 * mask : 2 * mask + 2] = part[...]


def krylov_kernel(team, size, emb_width, place_ref, noise, *refs):
    *parts, out_ref, blocks, left, right, gram, start, vectors = refs
    order = size * BS
    rhs = start.shape[0]
    clusters = parts[0].shape[0]
    devices = team * clusters
    packed = [
        jnp.sum(place_ref[group : group + 1, :]).astype(jnp.int32) for group in range(devices // 4)
    ]
    places = [(packed[index // 4] >> (5 * (index % 4))) & 31 for index in range(devices)]
    for index in range(devices):
        member, chip = index % team, index // team
        mask, side = chip % (clusters // 2), chip // (clusters // 2)
        blocks[places[index]] = parts[member][2 * mask + side]
    lane = lax.broadcasted_iota(jnp.int32, (BS, LANES), 1)
    line = lax.broadcasted_iota(jnp.int32, (LANES, BS), 0)
    for place in range(size):
        tile = blocks[place]
        rows = slice(place * BS, (place + 1) * BS)
        emb = tile[:BS].astype(F32)
        turned = emb.T
        left[rows, :emb_width] = tile[:BS]
        right[:emb_width, rows] = (turned * -2.0).astype(BF16)
        top, middle, low = split3(jnp.sum(emb * emb, axis=1, keepdims=True))
        extra = jnp.where(lane < 2 * 3, 1.0, 0.0)
        extra = jnp.where(lane == 2, low, extra)
        extra = jnp.where(lane == 1, middle, extra)
        left[rows, emb_width:] = jnp.where(lane == 0, top, extra).astype(BF16)
        top, middle, low = split3(jnp.sum(turned * turned, axis=0, keepdims=True))
        extra = jnp.where(line < 3, 1.0, 0.0)
        extra = jnp.where(line == 5, low, extra)
        extra = jnp.where(line == 4, middle, extra)
        right[emb_width:, rows] = jnp.where(line == 3, top, extra).astype(BF16)
        start[:, rows] = tile[BS : BS + rhs].astype(F32)

    rate = math.sqrt(5.0) / (0.5 * math.sqrt(2.0 * emb_width))
    chunk = 256
    for column in range(0, order, chunk):
        columns = slice(column, column + chunk)
        distance_sq = jnp.dot(
            left[: column + chunk, :], right[:, columns], preferred_element_type=F32
        )
        distance_sq = jnp.maximum(distance_sq, 1e-12)
        distance = distance_sq * lax.rsqrt(distance_sq)
        value = (distance * (rate * rate / 3.0) + rate) * distance + 1.0
        value = (value * jnp.exp2(distance * (-rate * math.log2(math.e)))).astype(BF16)
        gram[: column + chunk, columns] = value
        for above in range(0, column, chunk):
            gram[columns, above : above + chunk] = value[above : above + chunk].T

    basis, numbers, scales = [start[...]], [], []
    for step in range(STEPS):
        vector = basis[step]
        image = jnp.dot(vector.astype(BF16), gram[...], preferred_element_type=F32)
        square = jnp.sum(vector * vector, axis=1, keepdims=True)
        scales.append(jnp.where(square > 0.0, 1.0 / square, 0.0))
        image = image + noise[...] * vector
        parts_of = [
            jnp.sum(one * image, axis=1, keepdims=True) * scale
            for one, scale in zip(basis, scales, strict=True)
        ]
        for one, part in zip(basis, parts_of, strict=True):
            image = image - part * one
        basis.append(image)
        vectors[step * rhs : (step + 1) * rhs, :order] = image.astype(BF16)
        numbers += [square] + parts_of

    spot = lax.broadcasted_iota(jnp.int32, (rhs, LANES), 1)
    table = jnp.zeros((rhs, LANES), F32)
    for index, number in enumerate(numbers):
        table = jnp.where(spot == index, number, table)
    table = jnp.concatenate([table, jnp.zeros((LANES - rhs, LANES), F32)], axis=0).T[:16]
    top, middle, low = split3(table)
    table = top + pltpu.roll(middle, rhs, 1) + pltpu.roll(low, 2 * rhs, 1)
    table = table.astype(BF16)
    for slot in range(out_ref.shape[0]):
        out_ref[slot, STEPS * rhs : (STEPS + 1) * rhs, :] = table
    chip = lax.axis_index("rows") // team
    for other in range(devices // team):
        at = pl.ds(pl.multiple_of(places[other * team] * BS, BS), BS)
        out_ref[chip ^ other, : STEPS * rhs, :] = vectors[:, at]


def combine_kernel(label_ref, back_ref, rhs_ref, solution_ref, residual_ref, table):
    clusters = back_ref.shape[0]
    rhs = rhs_ref.shape[0]
    for cluster in range(clusters):
        part = back_ref[cluster, STEPS * rhs : STEPS * rhs + 16, :].astype(F32)
        table[cluster] = (
            part + pltpu.roll(part, LANES - rhs, 1) + pltpu.roll(part, LANES - 2 * rhs, 1)
        )
    squares, mixing, at = [], [], 0
    for step in range(STEPS):
        squares.append(table[:, at, :])
        mixing.append([table[:, at + 1 + k, :] for k in range(step + 1)])
        at += step + 2
    one = jnp.ones_like(squares[0])
    solution, residual, direction = [], [one], [one]

    def total(values):
        return jnp.sum(functools.reduce(jnp.add, values), axis=0, keepdims=True)

    norm_now = total([squares[0]])
    for step in range(STEPS):
        image = []
        for out in range(step + 2):
            terms = [mixing[k][out] * direction[k] for k in range(out, step + 1)]
            image.append(functools.reduce(jnp.add, terms + direction[out - 1 : out]))
        step_len = norm_now / total(
            [squares[k] * direction[k] * image[k] for k in range(step + 1)]
        )
        solution = [x + step_len * p for x, p in zip(solution, direction)] + [
            step_len * direction[step]
        ]
        residual = [r - step_len * w for r, w in zip(residual, image)] + [-step_len * image[-1]]
        if step == STEPS - 1:
            break
        norm_next = total([squares[k] * residual[k] * residual[k] for k in range(step + 2)])
        ratio = norm_next / norm_now
        direction = [r + ratio * p for r, p in zip(residual, direction)] + [residual[-1]]
        norm_now = norm_next
    for index, coefficient in enumerate(solution + residual):
        table[:, index, :] = coefficient
    labels = labels_of(label_ref[:1, :], lax.axis_index("rows"))
    coefs = [table[label, 0:8, :] for label in labels]
    turned = jnp.concatenate(coefs + [jnp.zeros((LANES - 8 * BLK_DEV, LANES), F32)], axis=0).T
    for slot, label in enumerate(labels):
        block = slice(slot * BS, (slot + 1) * BS)
        vectors = [rhs_ref[:, block]] + [
            back_ref[label, step * rhs : (step + 1) * rhs, :].astype(F32) for step in range(STEPS)
        ]
        weights = [turned[:rhs, slot * 8 + k : slot * 8 + k + 1] for k in range(2 * STEPS + 1)]
        solution_ref[:, block] = functools.reduce(
            jnp.add, [weights[k] * vectors[k] for k in range(STEPS)]
        )
        residual_ref[:, block] = functools.reduce(
            jnp.add, [weights[STEPS + k] * vectors[k] for k in range(STEPS + 1)]
        )


def local(embeddings, noise_diag, right_side, pairs):
    devices = lax.axis_size("rows")
    emb_width = embeddings.shape[1]
    rhs, local_rows = right_side.shape
    count = pairs.shape[1]
    size = count // 2 - 1
    team = size // BLK_DEV
    clusters = devices // team
    order = size * BS
    width = pl.cdiv(devices * BLK_DEV, LANES) * LANES
    params = pltpu.CompilerParams(vmem_limit_bytes=48 * 1024 * 1024)

    def call(kernel, name, out_shape, args, scratch=(), cost=None, space=pltpu.VMEM):
        vmem = pl.BlockSpec(memory_space=pltpu.VMEM)
        return pl.pallas_call(
            kernel,
            out_shape=out_shape,
            in_specs=[pl.BlockSpec(memory_space=space)] * len(args),
            out_specs=jax.tree.map(lambda _: vmem, out_shape),
            scratch_shapes=scratch,
            compiler_params=params,
            cost_estimate=cost,
            name=name,
        )(*args)

    def swap(value, distance):
        return lax.ppermute(value, "rows", [(i, i ^ distance) for i in range(devices)])

    sources = [pairs, noise_diag.reshape(BLK_DEV, BS), embeddings, right_side]
    every, own = call(
        announce_kernel,
        "announce",
        (
            jax.ShapeDtypeStruct((devices, BLK_DEV, LANES), F32),
            jax.ShapeDtypeStruct((BLK_DEV, BS + rhs, LANES), BF16),
        ),
        [pltpu.with_memory_space_constraint(one, pltpu.HBM) for one in sources],
        scratch=[
            pltpu.VMEM((2, count), jnp.int32),
            pltpu.VMEM((BLK_DEV, BS), F32),
            pltpu.VMEM((rhs, local_rows), F32),
            pltpu.SemaphoreType.DMA((3 + BLK_DEV,)),
        ],
        space=pltpu.HBM,
    )
    far = swap(own, devices // 2)
    every = lax.all_to_all(every, "rows", split_axis=0, concat_axis=0, tiled=True)
    every, far = lax.optimization_barrier((every, far))
    pair = jax.ShapeDtypeStruct((2, BS + rhs, LANES), BF16)
    *packed, label = call(
        functools.partial(plan_kernel, team),
        "plan",
        [pair] * (clusters // 2) + [jax.ShapeDtypeStruct((8, width), F32)],
        [every, own, far],
    )
    packed = [one if mask == 0 else swap(one, team * mask) for mask, one in enumerate(packed)]
    place, noise = call(
        functools.partial(places_kernel, team, size),
        "places",
        (
            jax.ShapeDtypeStruct((max(8, devices // 4), LANES), F32),
            jax.ShapeDtypeStruct((1, order), F32),
        ),
        [label, every],
        cost=pl.CostEstimate(flops=10**6, bytes_accessed=10**6, transcendentals=0),
    )
    parts = [
        call(
            merge_kernel,
            "merge",
            jax.ShapeDtypeStruct((clusters, BS + rhs, LANES), BF16),
            [place, *packed],
        )
    ]
    reach = 1
    while reach < team:
        parts = parts + [swap(one, reach) for one in parts]
        reach *= 2
    back = call(
        functools.partial(krylov_kernel, team, size, emb_width),
        "krylov",
        jax.ShapeDtypeStruct((clusters, (STEPS + 1) * rhs, LANES), BF16),
        [place, noise, *parts],
        scratch=[
            pltpu.VMEM((size + 1, BS + rhs, LANES), BF16),
            pltpu.VMEM((order, 2 * emb_width), BF16),
            pltpu.VMEM((2 * emb_width, order), BF16),
            pltpu.VMEM((order, order), BF16),
            pltpu.VMEM((rhs, order), F32),
            pltpu.VMEM((STEPS * rhs, order + BS), BF16),
        ],
    )
    same = [[lead * team + member for lead in range(clusters)] for member in range(team)]
    back = lax.all_to_all(
        back, "rows", split_axis=0, concat_axis=0, tiled=True, axis_index_groups=same
    )
    out = jax.ShapeDtypeStruct((rhs, local_rows), F32)
    return call(
        combine_kernel,
        "combine",
        (out, out),
        [label, back, right_side],
        scratch=[pltpu.VMEM((clusters, 16, LANES), F32)],
    )


def solution(mesh):
    in_specs = (
        P(("groups", "rows"), None),
        P(("groups", "rows")),
        P(None, ("groups", "rows")),
        P(None, ("groups", "rows")),
    )
    out_specs = (P(None, ("groups", "rows")), P(None, ("groups", "rows")))
    return jax.shard_map(local, mesh=mesh, in_specs=in_specs, out_specs=out_specs, check_vma=False)
```

```python
import functools
import math

import jax
import jax.numpy as jnp
from jax import lax
from jax.experimental import pallas as pl
from jax.experimental.pallas import tpu as pltpu
from jax.sharding import PartitionSpec as P

BS = 128
BLK_DEV = 4
STEPS = 3
LANES = 128
F32 = jnp.float32
BF16 = jnp.bfloat16


def split3(value):
    high = value.astype(BF16).astype(F32)
    rest = value - high
    middle = rest.astype(BF16).astype(F32)
    return high, middle, rest - middle


def labels_of(label, device):
    slot = lax.broadcasted_iota(jnp.int32, label.shape, 1) - device * BLK_DEV
    weight = jnp.where(slot == 0, 1.0, 0.0)
    for other in range(1, BLK_DEV):
        weight = jnp.where(slot == other, 32.0**other, weight)
    packed = jnp.sum(label * weight).astype(jnp.int32)
    return [(packed >> (5 * other)) & 31 for other in range(BLK_DEV)]


def announce_kernel(
    pairs_hbm, noise_hbm, emb_hbm, rhs_hbm, out_ref, own_ref, pairs_ref, noise_ref, rhs_ref, arrived
):
    rhs = rhs_hbm.shape[0]
    moves = [(pairs_hbm, pairs_ref), (noise_hbm, noise_ref), (rhs_hbm, rhs_ref)]
    for slot in range(BLK_DEV):
        moves.append((emb_hbm.at[slot * BS : (slot + 1) * BS, :], own_ref.at[slot, :BS, :]))
    fetches = [
        pltpu.make_async_copy(source, target, arrived.at[index])
        for index, (source, target) in enumerate(moves)
    ]
    for fetch in fetches:
        fetch.start()
    devices, height, _ = out_ref.shape
    lane = lax.broadcasted_iota(jnp.int32, (2, LANES), 1)
    line = lax.broadcasted_iota(jnp.int32, (height, LANES), 0)
    sign = jnp.ones((height, LANES), F32)
    fetches[0].wait()
    ids = pairs_ref[...]
    for row in range(pl.cdiv(devices * BLK_DEV, LANES)):
        hit = jnp.zeros((2, LANES), F32)
        for item in range(ids.shape[1]):
            hit = jnp.where(lane + row * LANES == ids[:, item : item + 1], 1.0, hit)
        named = jnp.max(hit, axis=0, keepdims=True)
        sign = jnp.where(jnp.logical_and(line == row, named > 0.0), -1.0, sign)
    fetches[1].wait()
    tile = (sign * noise_ref[...]).astype(BF16)
    for device in range(devices):
        out_ref[device] = tile
    fetches[2].wait()
    for slot in range(BLK_DEV):
        own_ref[slot, BS : BS + rhs, :] = rhs_ref[:, slot * BS : (slot + 1) * BS].astype(BF16)
    for fetch in fetches[3:]:
        fetch.wait()


def plan_kernel(team, news_ref, own_ref, far_ref, *outs):
    *packed_refs, label_ref = outs
    devices = news_ref.shape[0]
    width = pl.cdiv(devices * BLK_DEV, LANES) * LANES
    me = lax.axis_index("rows")
    news = news_ref[...].astype(F32)
    named = jnp.concatenate([news[:, line, :] for line in range(width // LANES)], axis=1)
    named = jnp.where(named < 0.0, 1.0, 0.0)
    flags = named.astype(BF16)
    together = lax.dot_general(flags, flags, (((1,), (1,)), ((), ())), preferred_element_type=F32)
    together = together > 0.0
    if team > 2:
        link = together.astype(F32).astype(BF16)
        together = jnp.dot(link, link, preferred_element_type=F32) > 0.0
    down = lax.broadcasted_iota(jnp.int32, (devices, devices), 0).astype(F32)
    across = lax.broadcasted_iota(jnp.int32, (devices, devices), 1).astype(F32)
    far = float(devices)
    leader_down = jnp.min(jnp.where(together, across, far), axis=1, keepdims=True)
    leader_across = jnp.min(jnp.where(together, down, far), axis=0, keepdims=True)
    first = leader_across == across
    rank = jnp.sum(
        jnp.where(jnp.logical_and(first, across < leader_down), 1.0, 0.0), axis=1, keepdims=True
    )
    label = jnp.max(named * rank, axis=0, keepdims=True)

    label_ref[...] = jnp.broadcast_to(label, label_ref.shape)
    far = me ^ (devices // 2)
    sources = [(own_ref, labels_of(label, me)), (far_ref, labels_of(label, far))]
    for mask, packed_ref in enumerate(packed_refs):
        target = (me // team) ^ mask
        for side, (blocks, labels) in enumerate(sources):
            packed_ref[side] = blocks[sum(jnp.where(labels[k] == target, k, 0) for k in range(1, BLK_DEV))]


def news_of(rows, index):
    line = lax.broadcasted_iota(jnp.int32, rows.shape, 0)
    picked = jnp.where(line == index, jnp.abs(rows.astype(F32)), 0.0)
    return jnp.sum(picked, axis=0, keepdims=True)


def places_kernel(team, size, label_ref, news_ref, place_ref, noise_ref):
    devices = news_ref.shape[0]
    height, width = label_ref.shape
    me = lax.axis_index("rows")
    hit = jnp.where(label_ref[...] == (me // team).astype(F32), 1.0, 0.0)
    down = lax.broadcasted_iota(jnp.int32, (width, width), 0)
    across = lax.broadcasted_iota(jnp.int32, (width, width), 1)
    upper = jnp.where(down <= across, 1.0, 0.0).astype(BF16)
    before = jnp.dot(hit.astype(BF16), upper, preferred_element_type=F32)
    home = lax.broadcasted_iota(jnp.int32, (width, LANES), 0) // BLK_DEV
    relative = lax.broadcasted_iota(jnp.int32, (width, LANES), 1)
    chosen = jnp.where((home ^ me) == relative, 1.0, 0.0).astype(BF16)
    offset = (hit * (before - 1.0 - size)).astype(BF16)
    place = jnp.dot(offset, chosen, preferred_element_type=F32)[:1] + float(size)
    column = lax.broadcasted_iota(jnp.int32, place_ref.shape, 1)
    line = lax.broadcasted_iota(jnp.int32, place_ref.shape, 0)
    weight = jnp.where(column % 4 == 0, 1.0, jnp.where(column % 4 == 1, 32.0, 1024.0))
    weight = jnp.where(column % 4 == 3, 32768.0, weight)
    place_ref[...] = jnp.where(column // 4 == line, place * weight, 0.0)
    block_id = lax.broadcasted_iota(jnp.int32, (1, width), 1).astype(F32)
    for spot in range(size):
        here = jnp.logical_and(hit[:1] > 0.0, before[:1] == spot + 1.0)
        block = jnp.sum(jnp.where(here, block_id, 0.0)).astype(jnp.int32)
        noise_ref[:, spot * BS : (spot + 1) * BS] = news_of(
            news_ref[block // BLK_DEV], block % BLK_DEV
        )


def merge_kernel(place_ref, *refs):
    *parts, out_ref = refs
    for mask, part in enumerate(parts):
        out_ref[2 * mask : 2 * mask + 2] = part[...]


def krylov_kernel(team, size, emb_width, place_ref, noise, *refs):
    *parts, out_ref, blocks, left, right, gram, start, vectors = refs
    order = size * BS
    rhs = start.shape[0]
    clusters = parts[0].shape[0]
    devices = team * clusters
    packed = [
        jnp.sum(place_ref[group : group + 1, :]).astype(jnp.int32) for group in range(devices // 4)
    ]
    places = [(packed[index // 4] >> (5 * (index % 4))) & 31 for index in range(devices)]
    for index in range(devices):
        member, chip = index % team, index // team
        mask, side = chip % (clusters // 2), chip // (clusters // 2)
        blocks[places[index]] = parts[member][2 * mask + side]
    lane = lax.broadcasted_iota(jnp.int32, (BS, LANES), 1)
    line = lax.broadcasted_iota(jnp.int32, (LANES, BS), 0)
    for place in range(size):
        tile = blocks[place]
        rows = slice(place * BS, (place + 1) * BS)
        emb = tile[:BS].astype(F32)
        turned = emb.T
        left[rows, :emb_width] = tile[:BS]
        right[:emb_width, rows] = (turned * -2.0).astype(BF16)
        top, middle, low = split3(jnp.sum(emb * emb, axis=1, keepdims=True))
        extra = jnp.where(lane < 2 * 3, 1.0, 0.0)
        extra = jnp.where(lane == 2, low, extra)
        extra = jnp.where(lane == 1, middle, extra)
        left[rows, emb_width:] = jnp.where(lane == 0, top, extra).astype(BF16)
        top, middle, low = split3(jnp.sum(turned * turned, axis=0, keepdims=True))
        extra = jnp.where(line < 3, 1.0, 0.0)
        extra = jnp.where(line == 5, low, extra)
        extra = jnp.where(line == 4, middle, extra)
        right[emb_width:, rows] = jnp.where(line == 3, top, extra).astype(BF16)
        start[:, rows] = tile[BS : BS + rhs].astype(F32)

    rate = math.sqrt(5.0) / (0.5 * math.sqrt(2.0 * emb_width))
    chunk = 256
    for column in range(0, order, chunk):
        columns = slice(column, column + chunk)
        distance_sq = jnp.dot(
            left[: column + chunk, :], right[:, columns], preferred_element_type=F32
        )
        distance_sq = jnp.maximum(distance_sq, 1e-12)
        distance = distance_sq * lax.rsqrt(distance_sq)
        value = (distance * (rate * rate / 3.0) + rate) * distance + 1.0
        value = (value * jnp.exp2(distance * (-rate * math.log2(math.e)))).astype(BF16)
        gram[: column + chunk, columns] = value
        for above in range(0, column, chunk):
            gram[columns, above : above + chunk] = value[above : above + chunk].T

    basis, numbers, scales = [start[...]], [], []
    for step in range(STEPS):
        vector = basis[step]
        image = jnp.dot(vector.astype(BF16), gram[...], preferred_element_type=F32)
        square = jnp.sum(vector * vector, axis=1, keepdims=True)
        scales.append(jnp.where(square > 0.0, 1.0 / square, 0.0))
        image = image + noise[...] * vector
        parts_of = [
            jnp.sum(one * image, axis=1, keepdims=True) * scale
            for one, scale in zip(basis, scales, strict=True)
        ]
        for one, part in zip(basis, parts_of, strict=True):
            image = image - part * one
        basis.append(image)
        vectors[step * rhs : (step + 1) * rhs, :order] = image.astype(BF16)
        numbers += [square] + parts_of

    spot = lax.broadcasted_iota(jnp.int32, (rhs, LANES), 1)
    table = jnp.zeros((rhs, LANES), F32)
    for index, number in enumerate(numbers):
        table = jnp.where(spot == index, number, table)
    table = jnp.concatenate([table, jnp.zeros((LANES - rhs, LANES), F32)], axis=0).T[:16]
    top, middle, low = split3(table)
    table = top + pltpu.roll(middle, rhs, 1) + pltpu.roll(low, 2 * rhs, 1)
    table = table.astype(BF16)
    for slot in range(out_ref.shape[0]):
        out_ref[slot, STEPS * rhs : (STEPS + 1) * rhs, :] = table
    chip = lax.axis_index("rows") // team
    for other in range(devices // team):
        at = pl.ds(pl.multiple_of(places[other * team] * BS, BS), BS)
        out_ref[chip ^ other, : STEPS * rhs, :] = vectors[:, at]


def combine_kernel(label_ref, back_ref, rhs_ref, solution_ref, residual_ref, table):
    clusters = back_ref.shape[0]
    rhs = rhs_ref.shape[0]
    for cluster in range(clusters):
        part = back_ref[cluster, STEPS * rhs : STEPS * rhs + 16, :].astype(F32)
        table[cluster] = (
            part + pltpu.roll(part, LANES - rhs, 1) + pltpu.roll(part, LANES - 2 * rhs, 1)
        )
    squares, mixing, at = [], [], 0
    for step in range(STEPS):
        squares.append(table[:, at, :])
        mixing.append([table[:, at + 1 + k, :] for k in range(step + 1)])
        at += step + 2
    one = jnp.ones_like(squares[0])
    solution, residual, direction = [], [one], [one]

    def total(values):
        return jnp.sum(functools.reduce(jnp.add, values), axis=0, keepdims=True)

    norm_now = total([squares[0]])
    for step in range(STEPS):
        image = []
        for out in range(step + 2):
            terms = [mixing[k][out] * direction[k] for k in range(out, step + 1)]
            image.append(functools.reduce(jnp.add, terms + direction[out - 1 : out]))
        step_len = norm_now / total(
            [squares[k] * direction[k] * image[k] for k in range(step + 1)]
        )
        solution = [x + step_len * p for x, p in zip(solution, direction)] + [
            step_len * direction[step]
        ]
        residual = [r - step_len * w for r, w in zip(residual, image)] + [-step_len * image[-1]]
        if step == STEPS - 1:
            break
        norm_next = total([squares[k] * residual[k] * residual[k] for k in range(step + 2)])
        ratio = norm_next / norm_now
        direction = [r + ratio * p for r, p in zip(residual, direction)] + [residual[-1]]
        norm_now = norm_next
    for index, coefficient in enumerate(solution + residual):
        table[:, index, :] = coefficient
    labels = labels_of(label_ref[:1, :], lax.axis_index("rows"))
    coefs = [table[label, 0:8, :] for label in labels]
    turned = jnp.concatenate(coefs + [jnp.zeros((LANES - 8 * BLK_DEV, LANES), F32)], axis=0).T
    for slot, label in enumerate(labels):
        block = slice(slot * BS, (slot + 1) * BS)
        vectors = [rhs_ref[:, block]] + [
            back_ref[label, step * rhs : (step + 1) * rhs, :].astype(F32) for step in range(STEPS)
        ]
        weights = [turned[:rhs, slot * 8 + k : slot * 8 + k + 1] for k in range(2 * STEPS + 1)]
        solution_ref[:, block] = functools.reduce(
            jnp.add, [weights[k] * vectors[k] for k in range(STEPS)]
        )
        residual_ref[:, block] = functools.reduce(
            jnp.add, [weights[STEPS + k] * vectors[k] for k in range(STEPS + 1)]
        )


def local(embeddings, noise_diag, right_side, pairs):
    devices = lax.axis_size("rows")
    emb_width = embeddings.shape[1]
    rhs, local_rows = right_side.shape
    count = pairs.shape[1]
    size = count // 2 - 1
    team = size // BLK_DEV
    clusters = devices // team
    order = size * BS
    width = pl.cdiv(devices * BLK_DEV, LANES) * LANES
    params = pltpu.CompilerParams(vmem_limit_bytes=48 * 1024 * 1024)

    def call(kernel, name, out_shape, args, scratch=(), cost=None, space=pltpu.VMEM):
        vmem = pl.BlockSpec(memory_space=pltpu.VMEM)
        return pl.pallas_call(
            kernel,
            out_shape=out_shape,
            in_specs=[pl.BlockSpec(memory_space=space)] * len(args),
            out_specs=jax.tree.map(lambda _: vmem, out_shape),
            scratch_shapes=scratch,
            compiler_params=params,
            cost_estimate=cost,
            name=name,
        )(*args)

    def swap(value, distance):
        return lax.ppermute(value, "rows", [(i, i ^ distance) for i in range(devices)])

    sources = [pairs, noise_diag.reshape(BLK_DEV, BS), embeddings, right_side]
    every, own = call(
        announce_kernel,
        "announce",
        (
            jax.ShapeDtypeStruct((devices, BLK_DEV, LANES), BF16),
            jax.ShapeDtypeStruct((BLK_DEV, BS + rhs, LANES), BF16),
        ),
        [pltpu.with_memory_space_constraint(one, pltpu.HBM) for one in sources],
        scratch=[
            pltpu.VMEM((2, count), jnp.int32),
            pltpu.VMEM((BLK_DEV, BS), F32),
            pltpu.VMEM((rhs, local_rows), F32),
            pltpu.SemaphoreType.DMA((3 + BLK_DEV,)),
        ],
        space=pltpu.HBM,
    )
    far = swap(own, devices // 2)
    every = lax.all_to_all(every, "rows", split_axis=0, concat_axis=0, tiled=True)
    every, far = lax.optimization_barrier((every, far))
    pair = jax.ShapeDtypeStruct((2, BS + rhs, LANES), BF16)
    *packed, label = call(
        functools.partial(plan_kernel, team),
        "plan",
        [pair] * (clusters // 2) + [jax.ShapeDtypeStruct((8, width), F32)],
        [every, own, far],
    )
    packed = [one if mask == 0 else swap(one, team * mask) for mask, one in enumerate(packed)]
    place, noise = call(
        functools.partial(places_kernel, team, size),
        "places",
        (
            jax.ShapeDtypeStruct((max(8, devices // 4), LANES), F32),
            jax.ShapeDtypeStruct((1, order), F32),
        ),
        [label, every],
        cost=pl.CostEstimate(flops=10**6, bytes_accessed=10**6, transcendentals=0),
    )
    parts = [
        call(
            merge_kernel,
            "merge",
            jax.ShapeDtypeStruct((clusters, BS + rhs, LANES), BF16),
            [place, *packed],
        )
    ]
    reach = 1
    while reach < team:
        parts = parts + [swap(one, reach) for one in parts]
        reach *= 2
    back = call(
        functools.partial(krylov_kernel, team, size, emb_width),
        "krylov",
        jax.ShapeDtypeStruct((clusters, (STEPS + 1) * rhs, LANES), BF16),
        [place, noise, *parts],
        scratch=[
            pltpu.VMEM((size + 1, BS + rhs, LANES), BF16),
            pltpu.VMEM((order, 2 * emb_width), BF16),
            pltpu.VMEM((2 * emb_width, order), BF16),
            pltpu.VMEM((order, order), BF16),
            pltpu.VMEM((rhs, order), F32),
            pltpu.VMEM((STEPS * rhs, order + BS), BF16),
        ],
    )
    same = [[lead * team + member for lead in range(clusters)] for member in range(team)]
    back = lax.all_to_all(
        back, "rows", split_axis=0, concat_axis=0, tiled=True, axis_index_groups=same
    )
    out = jax.ShapeDtypeStruct((rhs, local_rows), F32)
    return call(
        combine_kernel,
        "combine",
        (out, out),
        [label, back, right_side],
        scratch=[pltpu.VMEM((clusters, 16, LANES), F32)],
    )


def solution(mesh):
    in_specs = (
        P(("groups", "rows"), None),
        P(("groups", "rows")),
        P(None, ("groups", "rows")),
        P(None, ("groups", "rows")),
    )
    out_specs = (P(None, ("groups", "rows")), P(None, ("groups", "rows")))
    return jax.shard_map(local, mesh=mesh, in_specs=in_specs, out_specs=out_specs, check_vma=False)
```

```python
import functools
import math

import jax
import jax.numpy as jnp
from jax import lax
from jax.experimental import pallas as pl
from jax.experimental.pallas import tpu as pltpu
from jax.sharding import PartitionSpec as P

BS = 128
BLK_DEV = 4
STEPS = 3
LANES = 128
F32 = jnp.float32
BF16 = jnp.bfloat16


def split3(value):
    high = value.astype(BF16).astype(F32)
    rest = value - high
    middle = rest.astype(BF16).astype(F32)
    return high, middle, rest - middle


def route(half):
    return [0, half - 1, *range(1, half - 1)]


def labels_of(label, device):
    slot = lax.broadcasted_iota(jnp.int32, label.shape, 1) - device * BLK_DEV
    weight = jnp.where(slot == 0, 1.0, 0.0)
    for other in range(1, BLK_DEV):
        weight = jnp.where(slot == other, 32.0**other, weight)
    packed = jnp.sum(label * weight).astype(jnp.int32)
    return [(packed >> (5 * other)) & 31 for other in range(BLK_DEV)]


def announce_kernel(
    pairs_hbm, noise_hbm, emb_hbm, rhs_hbm, out_ref, own_ref, pairs_ref, noise_ref, rhs_ref, arrived
):
    rhs = rhs_hbm.shape[0]
    moves = [(pairs_hbm, pairs_ref), (noise_hbm, noise_ref), (rhs_hbm, rhs_ref)]
    for slot in range(BLK_DEV):
        moves.append((emb_hbm.at[slot * BS : (slot + 1) * BS, :], own_ref.at[slot, :BS, :]))
    fetches = [
        pltpu.make_async_copy(source, target, arrived.at[index])
        for index, (source, target) in enumerate(moves)
    ]
    for fetch in fetches:
        fetch.start()
    devices, height, _ = out_ref.shape
    lane = lax.broadcasted_iota(jnp.int32, (2, LANES), 1)
    line = lax.broadcasted_iota(jnp.int32, (height, LANES), 0)
    sign = jnp.ones((height, LANES), F32)
    fetches[0].wait()
    ids = pairs_ref[...]
    for row in range(pl.cdiv(devices * BLK_DEV, LANES)):
        hit = jnp.zeros((2, LANES), F32)
        for item in range(ids.shape[1]):
            hit = jnp.where(lane + row * LANES == ids[:, item : item + 1], 1.0, hit)
        named = jnp.max(hit, axis=0, keepdims=True)
        sign = jnp.where(jnp.logical_and(line == row, named > 0.0), -1.0, sign)
    fetches[1].wait()
    tile = sign * noise_ref[...]
    for device in range(devices):
        out_ref[device] = tile
    fetches[2].wait()
    for slot in range(BLK_DEV):
        own_ref[slot, BS : BS + rhs, :] = rhs_ref[:, slot * BS : (slot + 1) * BS].astype(BF16)
    for fetch in fetches[3:]:
        fetch.wait()


def plan_kernel(team, news_ref, own_ref, far_ref, *outs):
    *packed_refs, label_ref = outs
    devices = news_ref.shape[0]
    width = pl.cdiv(devices * BLK_DEV, LANES) * LANES
    me = lax.axis_index("rows")
    named = jnp.concatenate([news_ref[:, line, :] for line in range(width // LANES)], axis=1)
    named = jnp.where(named < 0.0, 1.0, 0.0)
    flags = named.astype(BF16)
    together = lax.dot_general(flags, flags, (((1,), (1,)), ((), ())), preferred_element_type=F32)
    together = together > 0.0
    if team > 2:
        link = together.astype(F32).astype(BF16)
        together = jnp.dot(link, link, preferred_element_type=F32) > 0.0
    down = lax.broadcasted_iota(jnp.int32, (devices, devices), 0).astype(F32)
    across = lax.broadcasted_iota(jnp.int32, (devices, devices), 1).astype(F32)
    far = float(devices)
    leader_down = jnp.min(jnp.where(together, across, far), axis=1, keepdims=True)
    leader_across = jnp.min(jnp.where(together, down, far), axis=0, keepdims=True)
    first = leader_across == across
    rank = jnp.sum(
        jnp.where(jnp.logical_and(first, across < leader_down), 1.0, 0.0), axis=1, keepdims=True
    )
    label = jnp.max(named * rank, axis=0, keepdims=True)

    label_ref[...] = jnp.broadcast_to(label, label_ref.shape)
    far = me ^ (devices // 2)
    sources = [(own_ref, labels_of(label, me)), (far_ref, labels_of(label, far))]
    for mask, packed_ref in zip(route(len(packed_refs)), packed_refs, strict=True):
        target = (me // team) ^ mask
        for side, (blocks, labels) in enumerate(sources):
            packed_ref[side] = blocks[sum(jnp.where(labels[k] == target, k, 0) for k in range(1, BLK_DEV))]


def places_kernel(team, size, label_ref, news_ref, place_ref, noise_ref):
    devices = news_ref.shape[0]
    height, width = label_ref.shape
    me = lax.axis_index("rows")
    hit = jnp.where(label_ref[...] == (me // team).astype(F32), 1.0, 0.0)
    down = lax.broadcasted_iota(jnp.int32, (width, width), 0)
    across = lax.broadcasted_iota(jnp.int32, (width, width), 1)
    upper = jnp.where(down <= across, 1.0, 0.0).astype(BF16)
    before = jnp.dot(hit.astype(BF16), upper, preferred_element_type=F32)
    home = lax.broadcasted_iota(jnp.int32, (width, LANES), 0) // BLK_DEV
    relative = lax.broadcasted_iota(jnp.int32, (width, LANES), 1)
    chosen = jnp.where((home ^ me) == relative, 1.0, 0.0).astype(BF16)
    offset = (hit * (before - 1.0 - size)).astype(BF16)
    place = jnp.dot(offset, chosen, preferred_element_type=F32)[:1] + float(size)
    column = lax.broadcasted_iota(jnp.int32, place_ref.shape, 1)
    line = lax.broadcasted_iota(jnp.int32, place_ref.shape, 0)
    weight = jnp.where(column % 4 == 0, 1.0, jnp.where(column % 4 == 1, 32.0, 1024.0))
    weight = jnp.where(column % 4 == 3, 32768.0, weight)
    place_ref[...] = jnp.where(column // 4 == line, place * weight, 0.0)
    block_id = lax.broadcasted_iota(jnp.int32, (1, width), 1).astype(F32)
    for spot in range(size):
        here = jnp.logical_and(hit[:1] > 0.0, before[:1] == spot + 1.0)
        block = jnp.sum(jnp.where(here, block_id, 0.0)).astype(jnp.int32)
        noise_ref[:, spot * BS : (spot + 1) * BS] = jnp.abs(
            news_ref[block // BLK_DEV, pl.ds(block % BLK_DEV, 1), :]
        )


def merge_kernel(place_ref, *refs):
    *parts, out_ref = refs
    for mask, part in enumerate(parts):
        out_ref[2 * mask : 2 * mask + 2] = part[...]


def krylov_kernel(team, size, emb_width, place_ref, noise, *refs):
    *parts, out_ref, blocks, left, right, gram, start, vectors = refs
    order = size * BS
    rhs = start.shape[0]
    clusters = parts[0].shape[0]
    devices = team * clusters
    packed = [
        jnp.sum(place_ref[group : group + 1, :]).astype(jnp.int32) for group in range(devices // 4)
    ]
    places = [(packed[index // 4] >> (5 * (index % 4))) & 31 for index in range(devices)]
    for index in range(devices):
        member, chip = index % team, index // team
        mask, side = chip % (clusters // 2), chip // (clusters // 2)
        blocks[places[index]] = parts[member][2 * route(clusters // 2).index(mask) + side]
    lane = lax.broadcasted_iota(jnp.int32, (BS, LANES), 1)
    line = lax.broadcasted_iota(jnp.int32, (LANES, BS), 0)
    for place in range(size):
        tile = blocks[place]
        rows = slice(place * BS, (place + 1) * BS)
        emb = tile[:BS].astype(F32)
        turned = emb.T
        left[rows, :emb_width] = tile[:BS]
        right[:emb_width, rows] = (turned * -2.0).astype(BF16)
        top, middle, low = split3(jnp.sum(emb * emb, axis=1, keepdims=True))
        extra = jnp.where(lane < 2 * 3, 1.0, 0.0)
        extra = jnp.where(lane == 2, low, extra)
        extra = jnp.where(lane == 1, middle, extra)
        left[rows, emb_width:] = jnp.where(lane == 0, top, extra).astype(BF16)
        top, middle, low = split3(jnp.sum(turned * turned, axis=0, keepdims=True))
        extra = jnp.where(line < 3, 1.0, 0.0)
        extra = jnp.where(line == 5, low, extra)
        extra = jnp.where(line == 4, middle, extra)
        right[emb_width:, rows] = jnp.where(line == 3, top, extra).astype(BF16)
        start[:, rows] = tile[BS : BS + rhs].astype(F32)

    rate = math.sqrt(5.0) / (0.5 * math.sqrt(2.0 * emb_width))
    chunk = 256
    for column in range(0, order, chunk):
        columns = slice(column, column + chunk)
        distance_sq = jnp.dot(
            left[: column + chunk, :], right[:, columns], preferred_element_type=F32
        )
        distance_sq = jnp.maximum(distance_sq, 1e-12)
        distance = distance_sq * lax.rsqrt(distance_sq)
        value = (distance * (rate * rate / 3.0) + rate) * distance + 1.0
        value = (value * jnp.exp2(distance * (-rate * math.log2(math.e)))).astype(BF16)
        gram[: column + chunk, columns] = value
        for above in range(0, column, chunk):
            gram[columns, above : above + chunk] = value[above : above + chunk].T

    basis, numbers, scales = [start[...]], [], []
    for step in range(STEPS):
        vector = basis[step]
        image = jnp.dot(vector.astype(BF16), gram[...], preferred_element_type=F32)
        square = jnp.sum(vector * vector, axis=1, keepdims=True)
        scales.append(jnp.where(square > 0.0, 1.0 / square, 0.0))
        image = image + noise[...] * vector
        parts_of = [
            jnp.sum(one * image, axis=1, keepdims=True) * scale
            for one, scale in zip(basis, scales, strict=True)
        ]
        for one, part in zip(basis, parts_of, strict=True):
            image = image - part * one
        basis.append(image)
        vectors[step * rhs : (step + 1) * rhs, :order] = image.astype(BF16)
        numbers += [square] + parts_of

    spot = lax.broadcasted_iota(jnp.int32, (rhs, LANES), 1)
    table = jnp.zeros((rhs, LANES), F32)
    for index, number in enumerate(numbers):
        table = jnp.where(spot == index, number, table)
    table = jnp.concatenate([table, jnp.zeros((LANES - rhs, LANES), F32)], axis=0).T[:16]
    top, middle, low = split3(table)
    table = top + pltpu.roll(middle, rhs, 1) + pltpu.roll(low, 2 * rhs, 1)
    table = table.astype(BF16)
    for slot in range(out_ref.shape[0]):
        out_ref[slot, STEPS * rhs : (STEPS + 1) * rhs, :] = table
    chip = lax.axis_index("rows") // team
    for other in range(devices // team):
        at = pl.ds(pl.multiple_of(places[other * team] * BS, BS), BS)
        out_ref[chip ^ other, : STEPS * rhs, :] = vectors[:, at]


def combine_kernel(label_ref, back_ref, rhs_ref, solution_ref, residual_ref, table):
    clusters = back_ref.shape[0]
    rhs = rhs_ref.shape[0]
    for cluster in range(clusters):
        part = back_ref[cluster, STEPS * rhs : STEPS * rhs + 16, :].astype(F32)
        table[cluster] = (
            part + pltpu.roll(part, LANES - rhs, 1) + pltpu.roll(part, LANES - 2 * rhs, 1)
        )
    squares, mixing, at = [], [], 0
    for step in range(STEPS):
        squares.append(table[:, at, :])
        mixing.append([table[:, at + 1 + k, :] for k in range(step + 1)])
        at += step + 2
    one = jnp.ones_like(squares[0])
    solution, residual, direction = [], [one], [one]

    def total(values):
        return jnp.sum(functools.reduce(jnp.add, values), axis=0, keepdims=True)

    norm_now = total([squares[0]])
    for step in range(STEPS):
        image = []
        for out in range(step + 2):
            terms = [mixing[k][out] * direction[k] for k in range(out, step + 1)]
            image.append(functools.reduce(jnp.add, terms + direction[out - 1 : out]))
        step_len = norm_now / total(
            [squares[k] * direction[k] * image[k] for k in range(step + 1)]
        )
        solution = [x + step_len * p for x, p in zip(solution, direction)] + [
            step_len * direction[step]
        ]
        residual = [r - step_len * w for r, w in zip(residual, image)] + [-step_len * image[-1]]
        if step == STEPS - 1:
            break
        norm_next = total([squares[k] * residual[k] * residual[k] for k in range(step + 2)])
        ratio = norm_next / norm_now
        direction = [r + ratio * p for r, p in zip(residual, direction)] + [residual[-1]]
        norm_now = norm_next
    for index, coefficient in enumerate(solution + residual):
        table[:, index, :] = coefficient
    labels = labels_of(label_ref[:1, :], lax.axis_index("rows"))
    coefs = [table[label, 0:8, :] for label in labels]
    turned = jnp.concatenate(coefs + [jnp.zeros((LANES - 8 * BLK_DEV, LANES), F32)], axis=0).T
    for slot, label in enumerate(labels):
        block = slice(slot * BS, (slot + 1) * BS)
        vectors = [rhs_ref[:, block]] + [
            back_ref[label, step * rhs : (step + 1) * rhs, :].astype(F32) for step in range(STEPS)
        ]
        weights = [turned[:rhs, slot * 8 + k : slot * 8 + k + 1] for k in range(2 * STEPS + 1)]
        solution_ref[:, block] = functools.reduce(
            jnp.add, [weights[k] * vectors[k] for k in range(STEPS)]
        )
        residual_ref[:, block] = functools.reduce(
            jnp.add, [weights[STEPS + k] * vectors[k] for k in range(STEPS + 1)]
        )


def local(embeddings, noise_diag, right_side, pairs):
    devices = lax.axis_size("rows")
    emb_width = embeddings.shape[1]
    rhs, local_rows = right_side.shape
    count = pairs.shape[1]
    size = count // 2 - 1
    team = size // BLK_DEV
    clusters = devices // team
    order = size * BS
    width = pl.cdiv(devices * BLK_DEV, LANES) * LANES
    params = pltpu.CompilerParams(vmem_limit_bytes=48 * 1024 * 1024)

    def call(kernel, name, out_shape, args, scratch=(), cost=None, space=pltpu.VMEM):
        vmem = pl.BlockSpec(memory_space=pltpu.VMEM)
        return pl.pallas_call(
            kernel,
            out_shape=out_shape,
            in_specs=[pl.BlockSpec(memory_space=space)] * len(args),
            out_specs=jax.tree.map(lambda _: vmem, out_shape),
            scratch_shapes=scratch,
            compiler_params=params,
            cost_estimate=cost,
            name=name,
        )(*args)

    def swap(value, distance):
        return lax.ppermute(value, "rows", [(i, i ^ distance) for i in range(devices)])

    sources = [pairs, noise_diag.reshape(BLK_DEV, BS), embeddings, right_side]
    every, own = call(
        announce_kernel,
        "announce",
        (
            jax.ShapeDtypeStruct((devices, BLK_DEV, LANES), F32),
            jax.ShapeDtypeStruct((BLK_DEV, BS + rhs, LANES), BF16),
        ),
        [pltpu.with_memory_space_constraint(one, pltpu.HBM) for one in sources],
        scratch=[
            pltpu.VMEM((2, count), jnp.int32),
            pltpu.VMEM((BLK_DEV, BS), F32),
            pltpu.VMEM((rhs, local_rows), F32),
            pltpu.SemaphoreType.DMA((3 + BLK_DEV,)),
        ],
        space=pltpu.HBM,
    )
    far = swap(own, devices // 2)
    every = lax.all_to_all(every, "rows", split_axis=0, concat_axis=0, tiled=True)
    every, far = lax.optimization_barrier((every, far))
    pair = jax.ShapeDtypeStruct((2, BS + rhs, LANES), BF16)
    *packed, label = call(
        functools.partial(plan_kernel, team),
        "plan",
        [pair] * (clusters // 2) + [jax.ShapeDtypeStruct((8, width), F32)],
        [every, own, far],
    )
    packed = [
        one if mask == 0 else swap(one, team * mask)
        for mask, one in zip(route(clusters // 2), packed, strict=True)
    ]
    place, noise = call(
        functools.partial(places_kernel, team, size),
        "places",
        (
            jax.ShapeDtypeStruct((max(8, devices // 4), LANES), F32),
            jax.ShapeDtypeStruct((1, order), F32),
        ),
        [label, every],
        cost=pl.CostEstimate(flops=10**6, bytes_accessed=10**6, transcendentals=0),
    )
    parts = [
        call(
            merge_kernel,
            "merge",
            jax.ShapeDtypeStruct((clusters, BS + rhs, LANES), BF16),
            [place, *packed],
        )
    ]
    reach = 1
    while reach < team:
        parts = parts + [swap(one, reach) for one in parts]
        reach *= 2
    back = call(
        functools.partial(krylov_kernel, team, size, emb_width),
        "krylov",
        jax.ShapeDtypeStruct((clusters, (STEPS + 1) * rhs, LANES), BF16),
        [place, noise, *parts],
        scratch=[
            pltpu.VMEM((size + 1, BS + rhs, LANES), BF16),
            pltpu.VMEM((order, 2 * emb_width), BF16),
            pltpu.VMEM((2 * emb_width, order), BF16),
            pltpu.VMEM((order, order), BF16),
            pltpu.VMEM((rhs, order), F32),
            pltpu.VMEM((STEPS * rhs, order + BS), BF16),
        ],
    )
    same = [[lead * team + member for lead in range(clusters)] for member in range(team)]
    back = lax.all_to_all(
        back, "rows", split_axis=0, concat_axis=0, tiled=True, axis_index_groups=same
    )
    out = jax.ShapeDtypeStruct((rhs, local_rows), F32)
    return call(
        combine_kernel,
        "combine",
        (out, out),
        [label, back, right_side],
        scratch=[pltpu.VMEM((clusters, 16, LANES), F32)],
    )


def solution(mesh):
    in_specs = (
        P(("groups", "rows"), None),
        P(("groups", "rows")),
        P(None, ("groups", "rows")),
        P(None, ("groups", "rows")),
    )
    out_specs = (P(None, ("groups", "rows")), P(None, ("groups", "rows")))
    return jax.shard_map(local, mesh=mesh, in_specs=in_specs, out_specs=out_specs, check_vma=False)
```

```python
import functools
import math

import jax
import jax.numpy as jnp
from jax import lax
from jax.experimental import pallas as pl
from jax.experimental.pallas import tpu as pltpu
from jax.sharding import PartitionSpec as P

BS = 128
BLK_DEV = 4
STEPS = 3
LANES = 128
F32 = jnp.float32
BF16 = jnp.bfloat16


def split3(value):
    high = value.astype(BF16).astype(F32)
    rest = value - high
    middle = rest.astype(BF16).astype(F32)
    return high, middle, rest - middle


def route(half):
    return [0, half - 1, *range(1, half - 1)]


def labels_of(label, device):
    slot = lax.broadcasted_iota(jnp.int32, label.shape, 1) - device * BLK_DEV
    weight = jnp.where(slot == 0, 1.0, 0.0)
    for other in range(1, BLK_DEV):
        weight = jnp.where(slot == other, 32.0**other, weight)
    packed = jnp.sum(label * weight).astype(jnp.int32)
    return [(packed >> (5 * other)) & 31 for other in range(BLK_DEV)]


def announce_kernel(
    pairs_hbm, noise_hbm, emb_hbm, rhs_hbm, out_ref, own_ref, pairs_ref, noise_ref, rhs_ref, arrived
):
    rhs = rhs_hbm.shape[0]
    moves = [(pairs_hbm, pairs_ref), (noise_hbm, noise_ref), (rhs_hbm, rhs_ref)]
    for slot in range(BLK_DEV):
        moves.append((emb_hbm.at[slot * BS : (slot + 1) * BS, :], own_ref.at[slot, :BS, :]))
    fetches = [
        pltpu.make_async_copy(source, target, arrived.at[index])
        for index, (source, target) in enumerate(moves)
    ]
    for fetch in fetches:
        fetch.start()
    devices, height, _ = out_ref.shape
    lane = lax.broadcasted_iota(jnp.int32, (2, LANES), 1)
    line = lax.broadcasted_iota(jnp.int32, (height, LANES), 0)
    sign = jnp.ones((height, LANES), F32)
    fetches[0].wait()
    ids = pairs_ref[...]
    for row in range(pl.cdiv(devices * BLK_DEV, LANES)):
        hit = jnp.zeros((2, LANES), F32)
        for item in range(ids.shape[1]):
            hit = jnp.where(lane + row * LANES == ids[:, item : item + 1], 1.0, hit)
        named = jnp.max(hit, axis=0, keepdims=True)
        sign = jnp.where(jnp.logical_and(line == row, named > 0.0), -1.0, sign)
    fetches[1].wait()
    tile = (sign * noise_ref[...]).astype(BF16)
    for device in range(devices):
        out_ref[device] = tile
    fetches[2].wait()
    for slot in range(BLK_DEV):
        own_ref[slot, BS : BS + rhs, :] = rhs_ref[:, slot * BS : (slot + 1) * BS].astype(BF16)
    for fetch in fetches[3:]:
        fetch.wait()


def plan_kernel(team, news_ref, own_ref, far_ref, *outs):
    *packed_refs, label_ref = outs
    devices = news_ref.shape[0]
    width = pl.cdiv(devices * BLK_DEV, LANES) * LANES
    me = lax.axis_index("rows")
    news = news_ref[...].astype(F32)
    named = jnp.concatenate([news[:, line, :] for line in range(width // LANES)], axis=1)
    named = jnp.where(named < 0.0, 1.0, 0.0)
    flags = named.astype(BF16)
    together = lax.dot_general(flags, flags, (((1,), (1,)), ((), ())), preferred_element_type=F32)
    together = together > 0.0
    if team > 2:
        link = together.astype(F32).astype(BF16)
        together = jnp.dot(link, link, preferred_element_type=F32) > 0.0
    down = lax.broadcasted_iota(jnp.int32, (devices, devices), 0).astype(F32)
    across = lax.broadcasted_iota(jnp.int32, (devices, devices), 1).astype(F32)
    far = float(devices)
    leader_down = jnp.min(jnp.where(together, across, far), axis=1, keepdims=True)
    leader_across = jnp.min(jnp.where(together, down, far), axis=0, keepdims=True)
    first = leader_across == across
    rank = jnp.sum(
        jnp.where(jnp.logical_and(first, across < leader_down), 1.0, 0.0), axis=1, keepdims=True
    )
    label = jnp.max(named * rank, axis=0, keepdims=True)

    label_ref[...] = jnp.broadcast_to(label, label_ref.shape)
    far = me ^ (devices // 2)
    sources = [(own_ref, labels_of(label, me)), (far_ref, labels_of(label, far))]
    for mask, packed_ref in zip(route(len(packed_refs)), packed_refs, strict=True):
        target = (me // team) ^ mask
        for side, (blocks, labels) in enumerate(sources):
            packed_ref[side] = blocks[sum(jnp.where(labels[k] == target, k, 0) for k in range(1, BLK_DEV))]


def news_of(rows, index):
    line = lax.broadcasted_iota(jnp.int32, rows.shape, 0)
    picked = jnp.where(line == index, jnp.abs(rows.astype(F32)), 0.0)
    return jnp.sum(picked, axis=0, keepdims=True)


def places_kernel(team, size, label_ref, news_ref, place_ref, noise_ref):
    devices = news_ref.shape[0]
    height, width = label_ref.shape
    me = lax.axis_index("rows")
    hit = jnp.where(label_ref[...] == (me // team).astype(F32), 1.0, 0.0)
    down = lax.broadcasted_iota(jnp.int32, (width, width), 0)
    across = lax.broadcasted_iota(jnp.int32, (width, width), 1)
    upper = jnp.where(down <= across, 1.0, 0.0).astype(BF16)
    before = jnp.dot(hit.astype(BF16), upper, preferred_element_type=F32)
    home = lax.broadcasted_iota(jnp.int32, (width, LANES), 0) // BLK_DEV
    relative = lax.broadcasted_iota(jnp.int32, (width, LANES), 1)
    chosen = jnp.where((home ^ me) == relative, 1.0, 0.0).astype(BF16)
    offset = (hit * (before - 1.0 - size)).astype(BF16)
    place = jnp.dot(offset, chosen, preferred_element_type=F32)[:1] + float(size)
    column = lax.broadcasted_iota(jnp.int32, place_ref.shape, 1)
    line = lax.broadcasted_iota(jnp.int32, place_ref.shape, 0)
    weight = jnp.where(column % 4 == 0, 1.0, jnp.where(column % 4 == 1, 32.0, 1024.0))
    weight = jnp.where(column % 4 == 3, 32768.0, weight)
    place_ref[...] = jnp.where(column // 4 == line, place * weight, 0.0)
    block_id = lax.broadcasted_iota(jnp.int32, (1, width), 1).astype(F32)
    for spot in range(size):
        here = jnp.logical_and(hit[:1] > 0.0, before[:1] == spot + 1.0)
        block = jnp.sum(jnp.where(here, block_id, 0.0)).astype(jnp.int32)
        noise_ref[:, spot * BS : (spot + 1) * BS] = news_of(
            news_ref[block // BLK_DEV], block % BLK_DEV
        )


def merge_kernel(place_ref, *refs):
    *parts, out_ref = refs
    for mask, part in enumerate(parts):
        out_ref[2 * mask : 2 * mask + 2] = part[...]


def krylov_kernel(team, size, emb_width, place_ref, noise, *refs):
    *parts, out_ref, blocks, left, right, gram, start, vectors = refs
    order = size * BS
    rhs = start.shape[0]
    clusters = parts[0].shape[0]
    devices = team * clusters
    packed = [
        jnp.sum(place_ref[group : group + 1, :]).astype(jnp.int32) for group in range(devices // 4)
    ]
    places = [(packed[index // 4] >> (5 * (index % 4))) & 31 for index in range(devices)]
    for index in range(devices):
        member, chip = index % team, index // team
        mask, side = chip % (clusters // 2), chip // (clusters // 2)
        blocks[places[index]] = parts[member][2 * route(clusters // 2).index(mask) + side]
    lane = lax.broadcasted_iota(jnp.int32, (BS, LANES), 1)
    line = lax.broadcasted_iota(jnp.int32, (LANES, BS), 0)
    for place in range(size):
        tile = blocks[place]
        rows = slice(place * BS, (place + 1) * BS)
        emb = tile[:BS].astype(F32)
        turned = emb.T
        left[rows, :emb_width] = tile[:BS]
        right[:emb_width, rows] = (turned * -2.0).astype(BF16)
        top, middle, low = split3(jnp.sum(emb * emb, axis=1, keepdims=True))
        extra = jnp.where(lane < 2 * 3, 1.0, 0.0)
        extra = jnp.where(lane == 2, low, extra)
        extra = jnp.where(lane == 1, middle, extra)
        left[rows, emb_width:] = jnp.where(lane == 0, top, extra).astype(BF16)
        top, middle, low = split3(jnp.sum(turned * turned, axis=0, keepdims=True))
        extra = jnp.where(line < 3, 1.0, 0.0)
        extra = jnp.where(line == 5, low, extra)
        extra = jnp.where(line == 4, middle, extra)
        right[emb_width:, rows] = jnp.where(line == 3, top, extra).astype(BF16)
        start[:, rows] = tile[BS : BS + rhs].astype(F32)

    rate = math.sqrt(5.0) / (0.5 * math.sqrt(2.0 * emb_width))
    chunk = 256
    for column in range(0, order, chunk):
        columns = slice(column, column + chunk)
        distance_sq = jnp.dot(
            left[: column + chunk, :], right[:, columns], preferred_element_type=F32
        )
        distance_sq = jnp.maximum(distance_sq, 1e-12)
        distance = distance_sq * lax.rsqrt(distance_sq)
        value = (distance * (rate * rate / 3.0) + rate) * distance + 1.0
        value = (value * jnp.exp2(distance * (-rate * math.log2(math.e)))).astype(BF16)
        gram[: column + chunk, columns] = value
        for above in range(0, column, chunk):
            gram[columns, above : above + chunk] = value[above : above + chunk].T

    basis, numbers, scales = [start[...]], [], []
    for step in range(STEPS):
        vector = basis[step]
        image = jnp.dot(vector.astype(BF16), gram[...], preferred_element_type=F32)
        square = jnp.sum(vector * vector, axis=1, keepdims=True)
        scales.append(jnp.where(square > 0.0, 1.0 / square, 0.0))
        image = image + noise[...] * vector
        parts_of = [
            jnp.sum(one * image, axis=1, keepdims=True) * scale
            for one, scale in zip(basis, scales, strict=True)
        ]
        for one, part in zip(basis, parts_of, strict=True):
            image = image - part * one
        basis.append(image)
        vectors[step * rhs : (step + 1) * rhs, :order] = image.astype(BF16)
        numbers += [square] + parts_of

    spot = lax.broadcasted_iota(jnp.int32, (rhs, LANES), 1)
    table = jnp.zeros((rhs, LANES), F32)
    for index, number in enumerate(numbers):
        table = jnp.where(spot == index, number, table)
    table = jnp.concatenate([table, jnp.zeros((LANES - rhs, LANES), F32)], axis=0).T[:16]
    top, middle, low = split3(table)
    table = top + pltpu.roll(middle, rhs, 1) + pltpu.roll(low, 2 * rhs, 1)
    table = table.astype(BF16)
    for slot in range(out_ref.shape[0]):
        out_ref[slot, STEPS * rhs : (STEPS + 1) * rhs, :] = table
    chip = lax.axis_index("rows") // team
    for other in range(devices // team):
        at = pl.ds(pl.multiple_of(places[other * team] * BS, BS), BS)
        out_ref[chip ^ other, : STEPS * rhs, :] = vectors[:, at]


def combine_kernel(label_ref, back_ref, rhs_ref, solution_ref, residual_ref, table):
    clusters = back_ref.shape[0]
    rhs = rhs_ref.shape[0]
    for cluster in range(clusters):
        part = back_ref[cluster, STEPS * rhs : STEPS * rhs + 16, :].astype(F32)
        table[cluster] = (
            part + pltpu.roll(part, LANES - rhs, 1) + pltpu.roll(part, LANES - 2 * rhs, 1)
        )
    squares, mixing, at = [], [], 0
    for step in range(STEPS):
        squares.append(table[:, at, :])
        mixing.append([table[:, at + 1 + k, :] for k in range(step + 1)])
        at += step + 2
    one = jnp.ones_like(squares[0])
    solution, residual, direction = [], [one], [one]

    def total(values):
        return jnp.sum(functools.reduce(jnp.add, values), axis=0, keepdims=True)

    norm_now = total([squares[0]])
    for step in range(STEPS):
        image = []
        for out in range(step + 2):
            terms = [mixing[k][out] * direction[k] for k in range(out, step + 1)]
            image.append(functools.reduce(jnp.add, terms + direction[out - 1 : out]))
        step_len = norm_now / total(
            [squares[k] * direction[k] * image[k] for k in range(step + 1)]
        )
        solution = [x + step_len * p for x, p in zip(solution, direction)] + [
            step_len * direction[step]
        ]
        residual = [r - step_len * w for r, w in zip(residual, image)] + [-step_len * image[-1]]
        if step == STEPS - 1:
            break
        norm_next = total([squares[k] * residual[k] * residual[k] for k in range(step + 2)])
        ratio = norm_next / norm_now
        direction = [r + ratio * p for r, p in zip(residual, direction)] + [residual[-1]]
        norm_now = norm_next
    for index, coefficient in enumerate(solution + residual):
        table[:, index, :] = coefficient
    labels = labels_of(label_ref[:1, :], lax.axis_index("rows"))
    coefs = [table[label, 0:8, :] for label in labels]
    turned = jnp.concatenate(coefs + [jnp.zeros((LANES - 8 * BLK_DEV, LANES), F32)], axis=0).T
    for slot, label in enumerate(labels):
        block = slice(slot * BS, (slot + 1) * BS)
        vectors = [rhs_ref[:, block]] + [
            back_ref[label, step * rhs : (step + 1) * rhs, :].astype(F32) for step in range(STEPS)
        ]
        weights = [turned[:rhs, slot * 8 + k : slot * 8 + k + 1] for k in range(2 * STEPS + 1)]
        solution_ref[:, block] = functools.reduce(
            jnp.add, [weights[k] * vectors[k] for k in range(STEPS)]
        )
        residual_ref[:, block] = functools.reduce(
            jnp.add, [weights[STEPS + k] * vectors[k] for k in range(STEPS + 1)]
        )


def local(embeddings, noise_diag, right_side, pairs):
    devices = lax.axis_size("rows")
    emb_width = embeddings.shape[1]
    rhs, local_rows = right_side.shape
    count = pairs.shape[1]
    size = count // 2 - 1
    team = size // BLK_DEV
    clusters = devices // team
    order = size * BS
    width = pl.cdiv(devices * BLK_DEV, LANES) * LANES
    params = pltpu.CompilerParams(vmem_limit_bytes=48 * 1024 * 1024)

    def call(kernel, name, out_shape, args, scratch=(), cost=None, space=pltpu.VMEM):
        vmem = pl.BlockSpec(memory_space=pltpu.VMEM)
        return pl.pallas_call(
            kernel,
            out_shape=out_shape,
            in_specs=[pl.BlockSpec(memory_space=space)] * len(args),
            out_specs=jax.tree.map(lambda _: vmem, out_shape),
            scratch_shapes=scratch,
            compiler_params=params,
            cost_estimate=cost,
            name=name,
        )(*args)

    def swap(value, distance):
        return lax.ppermute(value, "rows", [(i, i ^ distance) for i in range(devices)])

    sources = [pairs, noise_diag.reshape(BLK_DEV, BS), embeddings, right_side]
    every, own = call(
        announce_kernel,
        "announce",
        (
            jax.ShapeDtypeStruct((devices, BLK_DEV, LANES), BF16),
            jax.ShapeDtypeStruct((BLK_DEV, BS + rhs, LANES), BF16),
        ),
        [pltpu.with_memory_space_constraint(one, pltpu.HBM) for one in sources],
        scratch=[
            pltpu.VMEM((2, count), jnp.int32),
            pltpu.VMEM((BLK_DEV, BS), F32),
            pltpu.VMEM((rhs, local_rows), F32),
            pltpu.SemaphoreType.DMA((3 + BLK_DEV,)),
        ],
        space=pltpu.HBM,
    )
    far = swap(own, devices // 2)
    every = lax.all_to_all(every, "rows", split_axis=0, concat_axis=0, tiled=True)
    every, far = lax.optimization_barrier((every, far))
    pair = jax.ShapeDtypeStruct((2, BS + rhs, LANES), BF16)
    *packed, label = call(
        functools.partial(plan_kernel, team),
        "plan",
        [pair] * (clusters // 2) + [jax.ShapeDtypeStruct((8, width), F32)],
        [every, own, far],
    )
    packed = [
        one if mask == 0 else swap(one, team * mask)
        for mask, one in zip(route(clusters // 2), packed, strict=True)
    ]
    place, noise = call(
        functools.partial(places_kernel, team, size),
        "places",
        (
            jax.ShapeDtypeStruct((max(8, devices // 4), LANES), F32),
            jax.ShapeDtypeStruct((1, order), F32),
        ),
        [label, every],
        cost=pl.CostEstimate(flops=10**6, bytes_accessed=10**6, transcendentals=0),
    )
    parts = [
        call(
            merge_kernel,
            "merge",
            jax.ShapeDtypeStruct((clusters, BS + rhs, LANES), BF16),
            [place, *packed],
        )
    ]
    reach = 1
    while reach < team:
        parts = parts + [swap(one, reach) for one in parts]
        reach *= 2
    back = call(
        functools.partial(krylov_kernel, team, size, emb_width),
        "krylov",
        jax.ShapeDtypeStruct((clusters, (STEPS + 1) * rhs, LANES), BF16),
        [place, noise, *parts],
        scratch=[
            pltpu.VMEM((size + 1, BS + rhs, LANES), BF16),
            pltpu.VMEM((order, 2 * emb_width), BF16),
            pltpu.VMEM((2 * emb_width, order), BF16),
            pltpu.VMEM((order, order), BF16),
            pltpu.VMEM((rhs, order), F32),
            pltpu.VMEM((STEPS * rhs, order + BS), BF16),
        ],
    )
    same = [[lead * team + member for lead in range(clusters)] for member in range(team)]
    back = lax.all_to_all(
        back, "rows", split_axis=0, concat_axis=0, tiled=True, axis_index_groups=same
    )
    out = jax.ShapeDtypeStruct((rhs, local_rows), F32)
    return call(
        combine_kernel,
        "combine",
        (out, out),
        [label, back, right_side],
        scratch=[pltpu.VMEM((clusters, 16, LANES), F32)],
    )


def solution(mesh):
    in_specs = (
        P(("groups", "rows"), None),
        P(("groups", "rows")),
        P(None, ("groups", "rows")),
        P(None, ("groups", "rows")),
    )
    out_specs = (P(None, ("groups", "rows")), P(None, ("groups", "rows")))
    return jax.shard_map(local, mesh=mesh, in_specs=in_specs, out_specs=out_specs, check_vma=False)
```

```python
import functools
import math

import jax
import jax.numpy as jnp
from jax import lax
from jax.experimental import pallas as pl
from jax.experimental.pallas import tpu as pltpu
from jax.sharding import PartitionSpec as P

BS = 128
BLK_DEV = 4
STEPS = 3
LANES = 128
F32 = jnp.float32
BF16 = jnp.bfloat16


def split3(value):
    high = value.astype(BF16).astype(F32)
    rest = value - high
    middle = rest.astype(BF16).astype(F32)
    return high, middle, rest - middle


def route(half):
    return [0, half - 1, *range(1, half - 1)]


def labels_of(label, device):
    slot = lax.broadcasted_iota(jnp.int32, label.shape, 1) - device * BLK_DEV
    weight = jnp.where(slot == 0, 1.0, 0.0)
    for other in range(1, BLK_DEV):
        weight = jnp.where(slot == other, 32.0**other, weight)
    packed = jnp.sum(label * weight).astype(jnp.int32)
    return [(packed >> (5 * other)) & 31 for other in range(BLK_DEV)]


def announce_kernel(
    pairs_hbm, noise_hbm, emb_hbm, rhs_hbm, out_ref, own_ref, pairs_ref, noise_ref, rhs_ref, arrived
):
    rhs = rhs_hbm.shape[0]
    moves = [(pairs_hbm, pairs_ref), (noise_hbm, noise_ref), (rhs_hbm, rhs_ref)]
    for slot in range(BLK_DEV):
        moves.append((emb_hbm.at[slot * BS : (slot + 1) * BS, :], own_ref.at[slot, :BS, :]))
    fetches = [
        pltpu.make_async_copy(source, target, arrived.at[index])
        for index, (source, target) in enumerate(moves)
    ]
    for fetch in fetches:
        fetch.start()
    devices, height, _ = out_ref.shape
    lane = lax.broadcasted_iota(jnp.int32, (2, LANES), 1)
    line = lax.broadcasted_iota(jnp.int32, (height, LANES), 0)
    sign = jnp.ones((height, LANES), F32)
    fetches[0].wait()
    ids = pairs_ref[...]
    for row in range(pl.cdiv(devices * BLK_DEV, LANES)):
        hit = jnp.zeros((2, LANES), F32)
        for item in range(ids.shape[1]):
            hit = jnp.where(lane + row * LANES == ids[:, item : item + 1], 1.0, hit)
        named = jnp.max(hit, axis=0, keepdims=True)
        sign = jnp.where(jnp.logical_and(line == row, named > 0.0), -1.0, sign)
    fetches[1].wait()
    tile = (sign * noise_ref[...]).astype(BF16)
    for device in range(devices):
        out_ref[device] = tile
    fetches[2].wait()
    for slot in range(BLK_DEV):
        own_ref[slot, BS : BS + rhs, :] = rhs_ref[:, slot * BS : (slot + 1) * BS].astype(BF16)
    for fetch in fetches[3:]:
        fetch.wait()


def plan_kernel(team, news_ref, own_ref, far_ref, *outs):
    *packed_refs, label_ref = outs
    devices = news_ref.shape[0]
    width = pl.cdiv(devices * BLK_DEV, LANES) * LANES
    me = lax.axis_index("rows")
    news = news_ref[...].astype(F32)
    named = jnp.concatenate([news[:, line, :] for line in range(width // LANES)], axis=1)
    named = jnp.where(named < 0.0, 1.0, 0.0)
    flags = named.astype(BF16)
    together = lax.dot_general(flags, flags, (((1,), (1,)), ((), ())), preferred_element_type=F32)
    together = together > 0.0
    if team > 2:
        link = together.astype(F32).astype(BF16)
        together = jnp.dot(link, link, preferred_element_type=F32) > 0.0
    down = lax.broadcasted_iota(jnp.int32, (devices, devices), 0).astype(F32)
    across = lax.broadcasted_iota(jnp.int32, (devices, devices), 1).astype(F32)
    far = float(devices)
    leader_down = jnp.min(jnp.where(together, across, far), axis=1, keepdims=True)
    leader_across = jnp.min(jnp.where(together, down, far), axis=0, keepdims=True)
    first = leader_across == across
    rank = jnp.sum(
        jnp.where(jnp.logical_and(first, across < leader_down), 1.0, 0.0), axis=1, keepdims=True
    )
    label = jnp.max(named * rank, axis=0, keepdims=True)

    label_ref[...] = jnp.broadcast_to(label, label_ref.shape)
    far = me ^ (devices // 2)
    sources = [(own_ref, labels_of(label, me)), (far_ref, labels_of(label, far))]
    for mask, packed_ref in zip(route(len(packed_refs)), packed_refs, strict=True):
        target = (me // team) ^ mask
        for side, (blocks, labels) in enumerate(sources):
            packed_ref[side] = blocks[sum(jnp.where(labels[k] == target, k, 0) for k in range(1, BLK_DEV))]


def news_of(rows, index):
    line = lax.broadcasted_iota(jnp.int32, rows.shape, 0)
    picked = jnp.where(line == index, jnp.abs(rows.astype(F32)), 0.0)
    return jnp.sum(picked, axis=0, keepdims=True)


def places_kernel(team, size, label_ref, news_ref, place_ref, noise_ref):
    devices = news_ref.shape[0]
    height, width = label_ref.shape
    me = lax.axis_index("rows")
    hit = jnp.where(label_ref[...] == (me // team).astype(F32), 1.0, 0.0)
    down = lax.broadcasted_iota(jnp.int32, (width, width), 0)
    across = lax.broadcasted_iota(jnp.int32, (width, width), 1)
    upper = jnp.where(down <= across, 1.0, 0.0).astype(BF16)
    before = jnp.dot(hit.astype(BF16), upper, preferred_element_type=F32)
    home = lax.broadcasted_iota(jnp.int32, (width, LANES), 0) // BLK_DEV
    relative = lax.broadcasted_iota(jnp.int32, (width, LANES), 1)
    chosen = jnp.where((home ^ me) == relative, 1.0, 0.0).astype(BF16)
    offset = (hit * (before - 1.0 - size)).astype(BF16)
    place = jnp.dot(offset, chosen, preferred_element_type=F32)[:1] + float(size)
    column = lax.broadcasted_iota(jnp.int32, place_ref.shape, 1)
    line = lax.broadcasted_iota(jnp.int32, place_ref.shape, 0)
    weight = jnp.where(column % 4 == 0, 1.0, jnp.where(column % 4 == 1, 32.0, 1024.0))
    weight = jnp.where(column % 4 == 3, 32768.0, weight)
    place_ref[...] = jnp.where(column // 4 == line, place * weight, 0.0)
    block_id = lax.broadcasted_iota(jnp.int32, (1, width), 1).astype(F32)
    for spot in range(size):
        here = jnp.logical_and(hit[:1] > 0.0, before[:1] == spot + 1.0)
        block = jnp.sum(jnp.where(here, block_id, 0.0)).astype(jnp.int32)
        noise_ref[:, spot * BS : (spot + 1) * BS] = news_of(
            news_ref[block // BLK_DEV], block % BLK_DEV
        )


def merge_kernel(place_ref, *refs):
    *parts, out_ref = refs
    for mask, part in enumerate(parts):
        out_ref[2 * mask : 2 * mask + 2] = part[...]


def krylov_kernel(team, size, emb_width, place_ref, noise, *refs):
    *parts, out_ref, blocks, left, right, gram, start, vectors = refs
    order = size * BS
    rhs = start.shape[0]
    heads = parts[team:]
    clusters = parts[0].shape[0] + 2
    devices = team * clusters
    packed = [
        jnp.sum(place_ref[group : group + 1, :]).astype(jnp.int32) for group in range(devices // 4)
    ]
    places = [(packed[index // 4] >> (5 * (index % 4))) & 31 for index in range(devices)]
    for index in range(devices):
        member, chip = index % team, index // team
        mask, side = chip % (clusters // 2), chip // (clusters // 2)
        at = 2 * route(clusters // 2).index(mask) + side
        blocks[places[index]] = heads[member][at] if at < 2 else parts[member][at - 2]
    lane = lax.broadcasted_iota(jnp.int32, (BS, LANES), 1)
    line = lax.broadcasted_iota(jnp.int32, (LANES, BS), 0)
    for place in range(size):
        tile = blocks[place]
        rows = slice(place * BS, (place + 1) * BS)
        emb = tile[:BS].astype(F32)
        turned = emb.T
        left[rows, :emb_width] = tile[:BS]
        right[:emb_width, rows] = (turned * -2.0).astype(BF16)
        top, middle, low = split3(jnp.sum(emb * emb, axis=1, keepdims=True))
        extra = jnp.where(lane < 2 * 3, 1.0, 0.0)
        extra = jnp.where(lane == 2, low, extra)
        extra = jnp.where(lane == 1, middle, extra)
        left[rows, emb_width:] = jnp.where(lane == 0, top, extra).astype(BF16)
        top, middle, low = split3(jnp.sum(turned * turned, axis=0, keepdims=True))
        extra = jnp.where(line < 3, 1.0, 0.0)
        extra = jnp.where(line == 5, low, extra)
        extra = jnp.where(line == 4, middle, extra)
        right[emb_width:, rows] = jnp.where(line == 3, top, extra).astype(BF16)
        start[:, rows] = tile[BS : BS + rhs].astype(F32)

    rate = math.sqrt(5.0) / (0.5 * math.sqrt(2.0 * emb_width))
    chunk = 256
    for column in range(0, order, chunk):
        columns = slice(column, column + chunk)
        distance_sq = jnp.dot(
            left[: column + chunk, :], right[:, columns], preferred_element_type=F32
        )
        distance_sq = jnp.maximum(distance_sq, 1e-12)
        distance = distance_sq * lax.rsqrt(distance_sq)
        value = (distance * (rate * rate / 3.0) + rate) * distance + 1.0
        value = (value * jnp.exp2(distance * (-rate * math.log2(math.e)))).astype(BF16)
        gram[: column + chunk, columns] = value
        for above in range(0, column, chunk):
            gram[columns, above : above + chunk] = value[above : above + chunk].T

    basis, numbers, scales = [start[...]], [], []
    for step in range(STEPS):
        vector = basis[step]
        image = jnp.dot(vector.astype(BF16), gram[...], preferred_element_type=F32)
        square = jnp.sum(vector * vector, axis=1, keepdims=True)
        scales.append(jnp.where(square > 0.0, 1.0 / square, 0.0))
        image = image + noise[...] * vector
        parts_of = [
            jnp.sum(one * image, axis=1, keepdims=True) * scale
            for one, scale in zip(basis, scales, strict=True)
        ]
        for one, part in zip(basis, parts_of, strict=True):
            image = image - part * one
        basis.append(image)
        vectors[step * rhs : (step + 1) * rhs, :order] = image.astype(BF16)
        numbers += [square] + parts_of

    spot = lax.broadcasted_iota(jnp.int32, (rhs, LANES), 1)
    table = jnp.zeros((rhs, LANES), F32)
    for index, number in enumerate(numbers):
        table = jnp.where(spot == index, number, table)
    table = jnp.concatenate([table, jnp.zeros((LANES - rhs, LANES), F32)], axis=0).T[:16]
    top, middle, low = split3(table)
    table = top + pltpu.roll(middle, rhs, 1) + pltpu.roll(low, 2 * rhs, 1)
    table = table.astype(BF16)
    for slot in range(out_ref.shape[0]):
        out_ref[slot, STEPS * rhs : (STEPS + 1) * rhs, :] = table
    chip = lax.axis_index("rows") // team
    for other in range(devices // team):
        at = pl.ds(pl.multiple_of(places[other * team] * BS, BS), BS)
        out_ref[chip ^ other, : STEPS * rhs, :] = vectors[:, at]


def combine_kernel(label_ref, back_ref, rhs_ref, solution_ref, residual_ref, table):
    clusters = back_ref.shape[0]
    rhs = rhs_ref.shape[0]
    for cluster in range(clusters):
        part = back_ref[cluster, STEPS * rhs : STEPS * rhs + 16, :].astype(F32)
        table[cluster] = (
            part + pltpu.roll(part, LANES - rhs, 1) + pltpu.roll(part, LANES - 2 * rhs, 1)
        )
    squares, mixing, at = [], [], 0
    for step in range(STEPS):
        squares.append(table[:, at, :])
        mixing.append([table[:, at + 1 + k, :] for k in range(step + 1)])
        at += step + 2
    one = jnp.ones_like(squares[0])
    solution, residual, direction = [], [one], [one]

    def total(values):
        return jnp.sum(functools.reduce(jnp.add, values), axis=0, keepdims=True)

    norm_now = total([squares[0]])
    for step in range(STEPS):
        image = []
        for out in range(step + 2):
            terms = [mixing[k][out] * direction[k] for k in range(out, step + 1)]
            image.append(functools.reduce(jnp.add, terms + direction[out - 1 : out]))
        step_len = norm_now / total(
            [squares[k] * direction[k] * image[k] for k in range(step + 1)]
        )
        solution = [x + step_len * p for x, p in zip(solution, direction)] + [
            step_len * direction[step]
        ]
        residual = [r - step_len * w for r, w in zip(residual, image)] + [-step_len * image[-1]]
        if step == STEPS - 1:
            break
        norm_next = total([squares[k] * residual[k] * residual[k] for k in range(step + 2)])
        ratio = norm_next / norm_now
        direction = [r + ratio * p for r, p in zip(residual, direction)] + [residual[-1]]
        norm_now = norm_next
    for index, coefficient in enumerate(solution + residual):
        table[:, index, :] = coefficient
    labels = labels_of(label_ref[:1, :], lax.axis_index("rows"))
    coefs = [table[label, 0:8, :] for label in labels]
    turned = jnp.concatenate(coefs + [jnp.zeros((LANES - 8 * BLK_DEV, LANES), F32)], axis=0).T
    for slot, label in enumerate(labels):
        block = slice(slot * BS, (slot + 1) * BS)
        vectors = [rhs_ref[:, block]] + [
            back_ref[label, step * rhs : (step + 1) * rhs, :].astype(F32) for step in range(STEPS)
        ]
        weights = [turned[:rhs, slot * 8 + k : slot * 8 + k + 1] for k in range(2 * STEPS + 1)]
        solution_ref[:, block] = functools.reduce(
            jnp.add, [weights[k] * vectors[k] for k in range(STEPS)]
        )
        residual_ref[:, block] = functools.reduce(
            jnp.add, [weights[STEPS + k] * vectors[k] for k in range(STEPS + 1)]
        )


def local(embeddings, noise_diag, right_side, pairs):
    devices = lax.axis_size("rows")
    emb_width = embeddings.shape[1]
    rhs, local_rows = right_side.shape
    count = pairs.shape[1]
    size = count // 2 - 1
    team = size // BLK_DEV
    clusters = devices // team
    order = size * BS
    width = pl.cdiv(devices * BLK_DEV, LANES) * LANES
    params = pltpu.CompilerParams(vmem_limit_bytes=48 * 1024 * 1024)

    def call(kernel, name, out_shape, args, scratch=(), cost=None, space=pltpu.VMEM):
        vmem = pl.BlockSpec(memory_space=pltpu.VMEM)
        return pl.pallas_call(
            kernel,
            out_shape=out_shape,
            in_specs=[pl.BlockSpec(memory_space=space)] * len(args),
            out_specs=jax.tree.map(lambda _: vmem, out_shape),
            scratch_shapes=scratch,
            compiler_params=params,
            cost_estimate=cost,
            name=name,
        )(*args)

    def swap(value, distance):
        return lax.ppermute(value, "rows", [(i, i ^ distance) for i in range(devices)])

    sources = [pairs, noise_diag.reshape(BLK_DEV, BS), embeddings, right_side]
    every, own = call(
        announce_kernel,
        "announce",
        (
            jax.ShapeDtypeStruct((devices, BLK_DEV, LANES), BF16),
            jax.ShapeDtypeStruct((BLK_DEV, BS + rhs, LANES), BF16),
        ),
        [pltpu.with_memory_space_constraint(one, pltpu.HBM) for one in sources],
        scratch=[
            pltpu.VMEM((2, count), jnp.int32),
            pltpu.VMEM((BLK_DEV, BS), F32),
            pltpu.VMEM((rhs, local_rows), F32),
            pltpu.SemaphoreType.DMA((3 + BLK_DEV,)),
        ],
        space=pltpu.HBM,
    )
    far = swap(own, devices // 2)
    every = lax.all_to_all(every, "rows", split_axis=0, concat_axis=0, tiled=True)
    every, far = lax.optimization_barrier((every, far))
    pair = jax.ShapeDtypeStruct((2, BS + rhs, LANES), BF16)
    *packed, label = call(
        functools.partial(plan_kernel, team),
        "plan",
        [pair] * (clusters // 2) + [jax.ShapeDtypeStruct((8, width), F32)],
        [every, own, far],
    )
    packed = [
        one if mask == 0 else swap(one, team * mask)
        for mask, one in zip(route(clusters // 2), packed, strict=True)
    ]
    place, noise = call(
        functools.partial(places_kernel, team, size),
        "places",
        (
            jax.ShapeDtypeStruct((max(8, devices // 4), LANES), F32),
            jax.ShapeDtypeStruct((1, order), F32),
        ),
        [label, every],
        cost=pl.CostEstimate(flops=10**6, bytes_accessed=10**6, transcendentals=0),
    )
    parts = [
        call(
            merge_kernel,
            "merge",
            jax.ShapeDtypeStruct((clusters - 2, BS + rhs, LANES), BF16),
            [place, *packed[1:]],
        )
    ]
    heads = packed[:1]
    reach = 1
    while reach < team:
        heads = heads + [swap(one, reach) for one in heads]
        parts = parts + [swap(one, reach) for one in parts]
        reach *= 2
    back = call(
        functools.partial(krylov_kernel, team, size, emb_width),
        "krylov",
        jax.ShapeDtypeStruct((clusters, (STEPS + 1) * rhs, LANES), BF16),
        [place, noise, *parts, *heads],
        scratch=[
            pltpu.VMEM((size + 1, BS + rhs, LANES), BF16),
            pltpu.VMEM((order, 2 * emb_width), BF16),
            pltpu.VMEM((2 * emb_width, order), BF16),
            pltpu.VMEM((order, order), BF16),
            pltpu.VMEM((rhs, order), F32),
            pltpu.VMEM((STEPS * rhs, order + BS), BF16),
        ],
    )
    same = [[lead * team + member for lead in range(clusters)] for member in range(team)]
    back = lax.all_to_all(
        back, "rows", split_axis=0, concat_axis=0, tiled=True, axis_index_groups=same
    )
    out = jax.ShapeDtypeStruct((rhs, local_rows), F32)
    return call(
        combine_kernel,
        "combine",
        (out, out),
        [label, back, right_side],
        scratch=[pltpu.VMEM((clusters, 16, LANES), F32)],
    )


def solution(mesh):
    in_specs = (
        P(("groups", "rows"), None),
        P(("groups", "rows")),
        P(None, ("groups", "rows")),
        P(None, ("groups", "rows")),
    )
    out_specs = (P(None, ("groups", "rows")), P(None, ("groups", "rows")))
    return jax.shard_map(local, mesh=mesh, in_specs=in_specs, out_specs=out_specs, check_vma=False)
```
